256 devices in a mesh: dec: 32 (over y, x, core), ch: 8 (over z).
Axes of the slice: x: 4, y: 4, z: 8, core: 2. Of those that a mesh axis runs over, the one named last changes fastest.
Arguments:
- frame_cotangent: bfloat16 [256, 160, 8192], P('dec', None, 'ch'), may hold values from -5 to 5
- rollout_utterance: int32 [256], P('dec'), may hold values from 0 to 31, as said below
- frame_offset: int32 [256], P('dec'), may hold values from 0 to 32
- utterance_frames: int32 [32], P('dec'), may hold values from 1 to 128, 3072 in all
- normed_input: bfloat16 [32, 128, 1024], P('dec', None, 'ch'), may hold values from -6 to 6
- expand_weight: bfloat16 [1024, 2, 1024], P(None, None, 'ch'), may hold values from -0.1875 to 0.1875
- depth_kernel: bfloat16 [9, 1024], P(None, 'ch'), may hold values from -2 to 2
- norm_scale: float32 [1024], P('ch'), may hold values from 0.1 to 1.9
- norm_shift: float32 [1024], P('ch'), may hold values from -3 to 3
- project_weight: bfloat16 [1024, 1024], replicated, may hold values from -0.1875 to 0.1875
- adapter_weight: bfloat16 [1024, 8192], P(None, 'ch'), may hold values from -0.0625 to 0.0625
Outputs:
- grad_stream: bfloat16 [32, 128, 1024], P('dec', None, 'ch')
- grad_normed: bfloat16 [32, 128, 1024], P('dec', None, 'ch')
The draws below stay inside these ranges and needn't reach their ends.
Inputs may be any that keep to these rules, and one draw needn't show every extreme that they name: `rollout_utterance`: each utterance is named by exactly 8 rollouts; utterances k * 1 to (k + 1) - 1 are owned by index k of dec; among the 8 rollouts of one index of dec at most 1 name utterances of one owner, and some owner is named exactly 1 times; the rollouts of index k of dec always name some utterance of the owner (k + 16) mod 32.
All inputs are finite; a program needn't handle non-finite values. No bound on the sum of `utterance_frames` on one device may be relied on, other than what follows from the above.
Results may differ from the reference program's by a relative error of at most 0.03.
Values may be sent and summed in bfloat16 or wider, within the bound.
A program may use at most 128 MiB of HBM per device.

```python
import math
import jax
import jax.numpy as jnp
import numpy as np
from jax import lax

D = 8192
C = 1024
K = 9
U_DEV = 1
F = 128
PROMPT = 32
SEQ = 160
UTT = 32
R_DEV = 8
ROLLOUTS = 256
ROUTE_CAP = 1
N_DEC = 32


def draw_rollout_utterance(key, part):
    total_slots = N_DEC * ROUTE_CAP
    shuffled_slots = jax.random.permutation(jax.random.fold_in(key, 11), total_slots).astype(jnp.int32)
    far_slot = jnp.argmax((shuffled_slots == N_DEC // 2).astype(jnp.int32)).astype(jnp.int32)
    chosen = jnp.roll(shuffled_slots, -far_slot)[:R_DEV].astype(jnp.int32)
    ranking = jnp.argsort(jnp.argsort(chosen)).astype(jnp.int32)
    offsets = chosen % N_DEC
    within = ranking % U_DEV
    devices = jnp.arange(N_DEC, dtype=jnp.int32)[:, None]
    owners = (devices + offsets[None, :]) % N_DEC
    utts = owners * U_DEV + within[None, :]
    keys = jax.random.split(jax.random.fold_in(key, 23), N_DEC)
    orders = jax.vmap(lambda single: jax.random.permutation(single, R_DEV))(keys)
    shuffled = jnp.take_along_axis(utts, orders.astype(jnp.int32), axis=1)
    return shuffled.reshape(ROLLOUTS).astype(jnp.int32)


def place_ends(values, own_key, least, largest):
    spot = [jax.random.randint(jax.random.fold_in(own_key, axis), (), 0, length) for axis, length in enumerate(values.shape)]
    main_axis = values.shape.index(max(values.shape))
    next_to = spot[:main_axis] + [(spot[main_axis] + 1) % values.shape[main_axis]] + spot[main_axis + 1:]
    return values.at[tuple(spot)].set(least).at[tuple(next_to)].set(largest)


def level_of(key, dims, cuts, low, largest):
    level = 1.0
    for axis_at, shards_of in cuts:
        draws = jax.random.uniform(jax.random.fold_in(jax.random.fold_in(key, 6), axis_at), (shards_of,), jnp.float32, low / len(cuts), largest / len(cuts))
        level = level * jnp.repeat(jnp.exp(draws), dims[axis_at] // shards_of).reshape((-1,) + (1,) * (len(dims) - 1 - axis_at))
    return level


def split_up(amount, total, most, skew):
    loads = [(1 << 20) // math.isqrt(grade ** skew) + 1 for grade in range(2, amount + 1)]
    rest, given = total - most - (amount - 1), [1] * (amount - 1)
    while rest > 0:
        movable = [i for i in range(amount - 1) if given[i] < most]
        whole, left = sum([loads[i] for i in movable]), rest
        for i in movable:
            extra = min(most - given[i], max(1, left * loads[i] // whole), rest)
            given[i] = given[i] + extra
            rest = rest - extra
    return np.array([most] + given)


def ragged_sizes(own_key, number_of, total, most, lean):
    if number_of == 2:
        one = jax.random.randint(own_key, (), max(1, total - most), min(most, total - 1) + 1)
        return jnp.stack([one, total - one])
    lengths = jnp.asarray(split_up(number_of, total, most, lean), jnp.int32)
    couples = (number_of - 1) // 2
    donor, sink = lengths[1:1 + 2 * couples:2], lengths[2:2 + 2 * couples:2]
    room = jnp.minimum(donor - 1, most - sink)
    passed = jax.random.randint(jax.random.fold_in(own_key, 1), (couples,), 0, 1 << 20) % (room + 1)
    lengths = lengths.at[1:1 + 2 * couples:2].set(donor - passed).at[2:2 + 2 * couples:2].set(sink + passed)
    return lengths[jax.random.permutation(jax.random.fold_in(own_key, 2), number_of)]


def scatter_about(key, shape, width, bound, cuts=(), held_as=jnp.bfloat16):
    gain = level_of(key, shape, cuts, -0.22, 0.18) if cuts else 1.0
    result = jax.random.normal(key, shape, jnp.float32) * width * gain
    return jnp.minimum(jnp.maximum(result, -bound), bound).astype(held_as)


def setup_inputs(seed: int = 0) -> dict:
    splits = jax.random.split(jax.random.key(seed), 12)
    frame_cotangent = scatter_about(splits[0], (ROLLOUTS, SEQ, D), 0.35, 5.0, ((0, 32), (2, 8)))
    rollout_utterance = draw_rollout_utterance(jax.random.fold_in(splits[11], 71), 0)
    frame_offset = place_ends(jax.random.randint(splits[2], (ROLLOUTS,), 0, PROMPT + 1), jax.random.fold_in(splits[2], 1), 0, PROMPT).astype(jnp.int32)
    utterance_frames = ragged_sizes(splits[3], UTT, UTT * F * 3 // 4, F, 1).astype(jnp.int32)
    normed_input = scatter_about(splits[4], (UTT, F, C), 1.0, 6.0, ((0, 32), (2, 8)))
    expand_weight = scatter_about(splits[5], (C, 2, C), C ** -0.5, 0.1875, ((2, 8),))
    depth_kernel = scatter_about(splits[6], (K, C), K ** -0.5, 2.0, ((1, 8),))
    norm_scale = jnp.clip(1.0 + 0.18 * jax.random.normal(splits[7], (C,), jnp.float32), 0.1, 1.9)
    norm_shift = scatter_about(splits[8], (C,), 0.5, 3.0, ((0, 8),), jnp.float32)
    project_weight = scatter_about(splits[9], (C, C), C ** -0.5, 0.1875)
    adapter_weight = scatter_about(splits[10], (C, D), D ** -0.5, 0.0625, ((1, 8),))
    return {"frame_cotangent": frame_cotangent, "rollout_utterance": rollout_utterance, "frame_offset": frame_offset, "utterance_frames": utterance_frames, "normed_input": normed_input, "expand_weight": expand_weight, "depth_kernel": depth_kernel, "norm_scale": norm_scale, "norm_shift": norm_shift, "project_weight": project_weight, "adapter_weight": adapter_weight}


def reference(frame_cotangent, rollout_utterance, frame_offset, utterance_frames, normed_input, expand_weight, depth_kernel, norm_scale, norm_shift, project_weight, adapter_weight):
    grouped = frame_cotangent.reshape(N_DEC, R_DEV, SEQ, D)
    starts = frame_offset.astype(jnp.int32).reshape(N_DEC, R_DEV)
    owners = rollout_utterance.astype(jnp.int32).reshape(N_DEC, R_DEV)

    def per_device(total, item):
        rows, begin, utts = item
        slabs = jax.vmap(lambda window, first: lax.dynamic_slice_in_dim(window, first, F, 0))(rows, begin)
        part = jax.ops.segment_sum(slabs.astype(jnp.float32), utts, num_segments=UTT)
        rounded = lax.optimization_barrier(part.astype(jnp.bfloat16))
        return total + rounded.astype(jnp.float32), None

    total, _ = lax.scan(per_device, jnp.zeros((UTT, F, D), jnp.float32), (grouped, starts, owners))
    mask = (jnp.arange(F, dtype=jnp.int32)[None, :] < utterance_frames.astype(jnp.int32)[:, None]).astype(jnp.float32)
    frame_grad = (total * mask[:, :, None]).astype(jnp.bfloat16)
    grad_stream = jnp.dot(frame_grad.reshape(UTT * F, D), adapter_weight.T, preferred_element_type=jnp.float32).astype(jnp.bfloat16)

    expand_flat = expand_weight.reshape(C, 2 * C)
    expanded = jnp.dot(normed_input.reshape(UTT * F, C), expand_flat, preferred_element_type=jnp.float32)
    value = expanded[:, :C]
    gate = expanded[:, C:]
    sig_gate = jax.nn.sigmoid(gate)
    mask_rows = mask.reshape(UTT * F, 1)
    glu = (mask_rows * value * sig_gate).reshape(UTT, F, C)
    kernel = depth_kernel.astype(jnp.float32)
    half = (K - 1) // 2
    padded = jnp.pad(glu, ((0, 0), (half, half), (0, 0)))
    depth = jnp.zeros((UTT, F, C), jnp.float32)
    for k in range(K):
        depth = depth + kernel[k] * padded[:, k:k + F, :]
    shifted = depth * norm_scale + norm_shift
    grad_swish = jnp.dot(grad_stream, project_weight.T, preferred_element_type=jnp.float32).reshape(UTT, F, C)
    sig_shift = jax.nn.sigmoid(shifted)
    grad_depth = grad_swish * sig_shift * (1.0 + shifted * (1.0 - sig_shift)) * norm_scale
    padded_back = jnp.pad(grad_depth, ((0, 0), (half, half), (0, 0)))
    grad_glu = jnp.zeros((UTT, F, C), jnp.float32)
    for k in range(K):
        grad_glu = grad_glu + kernel[k] * padded_back[:, K - 1 - k:K - 1 - k + F, :]
    grad_glu = grad_glu.reshape(UTT * F, C) * mask_rows
    grad_value = grad_glu * sig_gate
    grad_gate = grad_glu * value * sig_gate * (1.0 - sig_gate)
    grad_expanded = jnp.concatenate([grad_value, grad_gate], axis=1).astype(jnp.bfloat16)
    grad_normed = jnp.dot(grad_expanded, expand_flat.T, preferred_element_type=jnp.float32).astype(jnp.bfloat16)
    return grad_stream.reshape(UTT, F, C), grad_normed.reshape(UTT, F, C)
```

```python
import jax
import jax.numpy as jnp
from jax import lax
from jax.experimental import pallas as pl
from jax.experimental.pallas import tpu as pltpu
from jax.sharding import PartitionSpec as P

MESH = pl.DeviceIdType.MESH
F32 = jnp.float32
BF16 = jnp.bfloat16
NY, NX, NCORE, NZ = 4, 4, 2, 8
RING = NX * NCORE


def steps(first, last, work):
    def one(step, carry):
        work(step)
        return carry

    lax.fori_loop(first, last, one, 0)


def rows_of(start, size):
    return pl.ds(pl.multiple_of(start, size), size)


def nt(a, b):
    return lax.dot_general(a, b, (((1,), (1,)), ((), ())), preferred_element_type=F32)


def kernel(
    ids_sm,
    offs_sm,
    frames_sm,
    normed_ref,
    taps_ref,
    scale_ref,
    shift_ref,
    cot_hbm,
    expand_hbm,
    project_hbm,
    adapter_hbm,
    stream_out,
    normed_out,
    cot,
    expand2,
    project,
    adapter,
    fused,
    expand,
    slabs,
    landed,
    ids,
    sel_t,
    sel,
    part,
    part_in,
    fg,
    x_all,
    zsend,
    zrecv,
    owned,
    back,
    pad,
    f_gsw,
    f_val,
    f_gate,
    load_sem,
    s1_send,
    s1_recv,
    id_send,
    id_recv,
    s2_send,
    s2_recv,
    z_send,
    z_recv,
    b_send,
    b_recv,
):
    me = lax.axis_index("dec")
    c = lax.axis_index("ch")
    y = lax.div(me, RING)
    pos_a = lax.rem(me, RING)
    x = lax.div(pos_a, NCORE)
    core = lax.rem(pos_a, NCORE)
    pos_b = y * NCORE + core
    positions = (pos_a, pos_b)

    def ring_dev(half, g):
        if half == 0:
            return y * RING + g
        return lax.div(g, NCORE) * RING + x * NCORE + lax.rem(g, NCORE)

    def line_dev(half, q):
        if half == 0:
            return q * RING + pos_a
        return y * RING + q * NCORE + core

    lines = (y, x)

    loads = []
    for r in range(8):
        loads.append(pltpu.make_async_copy(cot_hbm.at[r], cot.at[r], load_sem.at[r]))
    loads.append(pltpu.make_async_copy(project_hbm, project, load_sem.at[8]))
    loads.append(pltpu.make_async_copy(adapter_hbm, adapter, load_sem.at[9]))
    loads.append(pltpu.make_async_copy(expand_hbm, expand2, load_sem.at[10]))
    for load in loads:
        load.start()

    barrier = pltpu.get_barrier_semaphore()

    def greet(device):
        pl.semaphore_signal(barrier, inc=1, device_id=device, device_id_type=MESH)

    steps(1, RING, lambda o: greet((ring_dev(0, lax.rem(pos_a + o, RING)), c)))
    for other in range(NCORE):
        steps(1, NY, lambda o: greet((ring_dev(1, lax.rem(y + o, NY) * NCORE + other), c)))
    steps(1, NZ, lambda o: greet((me, lax.rem(c + o, NZ))))

    row8 = lax.broadcasted_iota(jnp.int32, (8, 128), 0)
    tile = jnp.zeros((8, 128), jnp.int32)
    for r in range(8):
        tile = jnp.where(row8 == r, ids_sm[r], tile)
    ids[0, pos_a] = tile
    ids[1, pos_b] = tile

    srow = lax.broadcasted_iota(jnp.int32, (128, 160), 0)
    scol = lax.broadcasted_iota(jnp.int32, (128, 160), 1)
    diff = scol - srow
    for p in range(4):
        loads[2 * p].wait()
        loads[2 * p + 1].wait()
        sh0 = (diff == offs_sm[2 * p]).astype(F32).astype(BF16)
        sh1 = (diff == offs_sm[2 * p + 1]).astype(F32).astype(BF16)
        for n in range(4):
            cols = slice(n * 256, (n + 1) * 256)
            a = jnp.dot(sh0, cot[2 * p, :, cols], preferred_element_type=F32)
            b = jnp.dot(sh1, cot[2 * p + 1, :, cols], preferred_element_type=F32)
            both = jnp.concatenate([a.reshape(16, 8, 256), b.reshape(16, 8, 256)], axis=1)
            slabs[:, p * 16 : (p + 1) * 16, cols] = both.astype(BF16)

    pl.semaphore_wait(barrier, 20)

    def s1_copy(half, g, slot):
        return pltpu.make_async_remote_copy(
            src_ref=slabs.at[half * 8 + g],
            dst_ref=landed.at[half, slot],
            send_sem=s1_send.at[half, g],
            recv_sem=s1_recv.at[half, slot],
            device_id=(ring_dev(half, g), c),
            device_id_type=MESH,
        )

    def id_copy(half, g, slot):
        return pltpu.make_async_remote_copy(
            src_ref=ids.at[half, positions[half]],
            dst_ref=ids.at[half, slot],
            send_sem=id_send.at[half, g],
            recv_sem=id_recv.at[half, slot],
            device_id=(ring_dev(half, g), c),
            device_id_type=MESH,
        )

    def s1_start(o):
        for half in range(2):
            g = lax.rem(positions[half] + o, RING)
            id_copy(half, g, positions[half]).start()
            s1_copy(half, g, positions[half]).start()

    steps(1, RING, s1_start)

    def z_copy(turn, src, dst, peer, slot):
        return pltpu.make_async_remote_copy(
            src_ref=src,
            dst_ref=dst.at[slot],
            send_sem=z_send.at[turn, peer],
            recv_sem=z_recv.at[turn, slot],
            device_id=(me, peer),
            device_id_type=MESH,
        )

    def x_copy(peer, slot):
        return z_copy(0, normed_ref, x_all, peer, slot)

    steps(1, NZ, lambda o: x_copy(lax.rem(c + o, NZ), c).start())
    x_all[c] = normed_ref[...]
    for half in range(2):
        landed[half, positions[half]] = slabs[half * 8 + positions[half]]

    loads[8].wait()
    loads[9].wait()

    def fuse(i):
        mine = rows_of(i * 128, 128)
        for n in range(4):
            cols = slice(n * 256, (n + 1) * 256)
            fused[mine, cols] = jnp.dot(
                project[mine, :], adapter[:, cols], preferred_element_type=F32
            ).astype(BF16)

    steps(0, 8, fuse)

    loads[10].wait()
    prow = lax.broadcasted_iota(jnp.int32, (256, 256), 0)
    pcol = lax.broadcasted_iota(jnp.int32, (256, 256), 1)
    want = jnp.where(prow < 128, 2 * prow, 2 * prow - 255)
    apart = (pcol == want).astype(F32).astype(BF16)
    for b in range(8):
        both = jnp.dot(apart, expand2[b * 256 : (b + 1) * 256, :], preferred_element_type=F32)
        both = both.astype(BF16)
        expand[b * 128 : (b + 1) * 128, 0:128] = both[:128]
        expand[b * 128 : (b + 1) * 128, 128:256] = both[128:]

    steps(1, NZ, lambda o: x_copy(lax.rem(c + o, NZ), lax.rem(c + o, NZ)).wait_recv())
    both = jnp.zeros((128, 256), F32)
    for b in range(8):
        both += jnp.dot(
            x_all[b], expand[b * 128 : (b + 1) * 128, :], preferred_element_type=F32
        )
    value = both[:, :128]
    sig_gate = jax.nn.sigmoid(both[:, 128:])
    frame = lax.broadcasted_iota(jnp.int32, (128, 128), 0)
    mask = (frame < frames_sm[0]).astype(F32)
    pad[...] = jnp.zeros_like(pad)
    pad[8:136, :] = mask * value * sig_gate
    taps = taps_ref[...].astype(F32)
    depth = jnp.zeros((128, 128), F32)
    for k in range(9):
        depth += taps[k : k + 1, :] * pad[4 + k : 132 + k, :]
    shifted = depth * scale_ref[...] + shift_ref[...]
    sig_shift = jax.nn.sigmoid(shifted)
    f_gsw[...] = sig_shift * (1.0 + shifted * (1.0 - sig_shift)) * scale_ref[...] * mask
    f_val[...] = sig_gate * mask
    f_gate[...] = value * sig_gate * (1.0 - sig_gate) * mask

    lane = lax.broadcasted_iota(jnp.int32, (8, 256), 1)
    same = lax.broadcasted_iota(jnp.int32, (8, 256), 0) == lax.rem(lane, 8)
    unit = lax.div(lane, 8)
    turned = (lax.rem(lax.div(unit, 2), 4) * NX + lax.div(unit, 8)) * NCORE + lax.rem(unit, 2)
    utts = (unit, turned)
    for half in range(2):

        def id_wait(o, half=half):
            slot = lax.rem(positions[half] + o, RING)
            id_copy(half, slot, slot).wait_recv()

        steps(1, RING, id_wait)

        def choose(s, half=half):
            for r in range(8):
                row = ids[half, s, r : r + 1, :]
                wide = jnp.concatenate([row, row], axis=1)
                hit = jnp.logical_and(same, wide == utts[half])
                sel_t[rows_of(s * 64 + r * 8, 8), :] = hit.astype(F32)

        steps(0, 8, choose)
        sel[half] = sel_t[...].T.astype(BF16)

    def s2_copy(half, q, slot):
        return pltpu.make_async_remote_copy(
            src_ref=part.at[half, q],
            dst_ref=part_in.at[half, slot],
            send_sem=s2_send.at[half, q],
            recv_sem=s2_recv.at[half, slot],
            device_id=(line_dev(half, q), c),
            device_id_type=MESH,
        )

    for half in range(2):

        def s1_wait(o, half=half):
            slot = lax.rem(positions[half] + o, RING)
            s1_copy(half, slot, slot).wait_recv()

        steps(1, RING, s1_wait)
        for n in range(4):
            cols = slice(n * 256, (n + 1) * 256)
            got = jnp.dot(
                sel[half],
                landed[half, :, :, cols].reshape(512, 256),
                preferred_element_type=F32,
            )
            part[half, :, :, cols] = got.astype(BF16).reshape(4, 64, 256)

        def s2_start(o, half=half):
            s2_copy(half, lax.rem(lines[half] + o, 4), lines[half]).start()

        steps(1, 4, s2_start)
        part_in[half, lines[half]] = part[half, lines[half]]

    for half in range(2):

        def s2_wait(o, half=half):
            slot = lax.rem(lines[half] + o, 4)
            s2_copy(half, slot, slot).wait_recv()

        steps(1, 4, s2_wait)
        total = part_in[half, 0].astype(F32)
        for q in range(1, 4):
            total += part_in[half, q].astype(F32)
        fg[half * 64 : (half + 1) * 64, :] = total.astype(BF16)

    for kind, weight in ((0, fused), (1, adapter)):
        for n in range(4):
            got = nt(fg[...], weight[n * 256 : (n + 1) * 256, :]).astype(BF16)
            zsend[kind, 2 * n] = got[:, :128]
            zsend[kind, 2 * n + 1] = got[:, 128:]

        def zk_start(o, kind=kind):
            peer = lax.rem(c + o, NZ)
            z_copy(1 + kind, zsend.at[kind, peer], zrecv.at[kind], peer, c).start()

        steps(1, NZ, zk_start)
        zrecv[kind, c] = zsend[kind, c]

    def back_copy(kind, half, g, slot):
        return pltpu.make_async_remote_copy(
            src_ref=owned.at[kind, rows_of(half * 64 + g * 8, 8), :],
            dst_ref=back.at[kind, rows_of(half * 64 + slot * 8, 8), :],
            send_sem=b_send.at[kind, half, g],
            recv_sem=b_recv.at[kind, half, slot],
            device_id=(ring_dev(half, g), c),
            device_id_type=MESH,
        )

    def z_sum(kind):
        def zk_wait(o):
            slot = lax.rem(c + o, NZ)
            z_copy(1 + kind, zsend.at[kind, slot], zrecv.at[kind], slot, slot).wait_recv()

        steps(1, NZ, zk_wait)
        total = zrecv[kind, 0].astype(F32)
        for b in range(1, NZ):
            total += zrecv[kind, b].astype(F32)
        return total

    def give_back(kind):
        owned[kind] = z_sum(kind)

        def go(o):
            for half in range(2):
                back_copy(kind, half, lax.rem(positions[half] + o, RING), positions[half]).start()

        steps(1, RING, go)
        for half in range(2):
            mine = rows_of(half * 64 + positions[half] * 8, 8)
            back[kind, mine, :] = owned[kind, mine, :]

    def back_wait(kind):
        def hold(o):
            for half in range(2):
                slot = lax.rem(positions[half] + o, RING)
                back_copy(kind, half, slot, slot).wait_recv()

        steps(1, RING, hold)

    give_back(0)
    back_wait(0)
    pad[8:136, :] = back[0] * f_gsw[...]
    grad_glu = jnp.zeros((128, 128), F32)
    for k in range(9):
        grad_glu += taps[k : k + 1, :] * pad[12 - k : 140 - k, :]
    grad_expanded = jnp.concatenate(
        [grad_glu * f_val[...], grad_glu * f_gate[...]], axis=1
    ).astype(BF16)
    for n in range(4):
        got = nt(grad_expanded, expand[n * 256 : (n + 1) * 256, :]).astype(BF16)
        zsend[2, 2 * n] = got[:, :128]
        zsend[2, 2 * n + 1] = got[:, 128:]

    def z2_start(o):
        peer = lax.rem(c + o, NZ)
        z_copy(3, zsend.at[2, peer], zrecv.at[2], peer, c).start()

    steps(1, NZ, z2_start)
    zrecv[2, c] = zsend[2, c]

    give_back(1)
    back_wait(1)
    stream_out[...] = (back[1] * mask).astype(BF16)
    normed_out[...] = z_sum(2).astype(BF16)

    def sent(o):
        peer = lax.rem(c + o, NZ)
        x_copy(peer, c).wait_send()
        for kind in range(3):
            z_copy(1 + kind, zsend.at[kind, peer], zrecv.at[kind], peer, c).wait_send()
        for half in range(2):
            g = lax.rem(positions[half] + o, RING)
            s1_copy(half, g, positions[half]).wait_send()
            id_copy(half, g, positions[half]).wait_send()
            for kind in range(2):
                back_copy(kind, half, g, positions[half]).wait_send()

    steps(1, NZ, sent)

    def sent_line(o):
        for half in range(2):
            s2_copy(half, lax.rem(lines[half] + o, 4), lines[half]).wait_send()

    steps(1, 4, sent_line)


def body(
    frame_cotangent,
    rollout_utterance,
    frame_offset,
    utterance_frames,
    normed_input,
    expand_weight,
    depth_kernel,
    norm_scale,
    norm_shift,
    project_weight,
    adapter_weight,
):
    smem = pl.BlockSpec(memory_space=pltpu.SMEM)
    vmem = pl.BlockSpec(memory_space=pltpu.VMEM)
    hbm = pl.BlockSpec(memory_space=pl.ANY)
    dma = pltpu.SemaphoreType.DMA
    block = jax.ShapeDtypeStruct((128, 128), BF16)
    stream, normed = pl.pallas_call(
        kernel,
        out_shape=(block, block),
        in_specs=[smem] * 3 + [vmem] * 4 + [hbm] * 4,
        out_specs=(vmem, vmem),
        scratch_shapes=[
            pltpu.VMEM((8, 160, 1024), BF16),
            pltpu.VMEM((2048, 128), BF16),
            pltpu.VMEM((1024, 1024), BF16),
            pltpu.VMEM((1024, 1024), BF16),
            pltpu.VMEM((1024, 1024), BF16),
            pltpu.VMEM((1024, 256), BF16),
            pltpu.VMEM((16, 64, 1024), BF16),
            pltpu.VMEM((2, 8, 64, 1024), BF16),
            pltpu.VMEM((2, 8, 8, 128), jnp.int32),
            pltpu.VMEM((512, 256), F32),
            pltpu.VMEM((2, 256, 512), BF16),
            pltpu.VMEM((2, 4, 64, 1024), BF16),
            pltpu.VMEM((2, 4, 64, 1024), BF16),
            pltpu.VMEM((128, 1024), BF16),
            pltpu.VMEM((8, 128, 128), BF16),
            pltpu.VMEM((3, 8, 128, 128), BF16),
            pltpu.VMEM((3, 8, 128, 128), BF16),
            pltpu.VMEM((2, 128, 128), F32),
            pltpu.VMEM((2, 128, 128), F32),
            pltpu.VMEM((144, 128), F32),
            pltpu.VMEM((128, 128), F32),
            pltpu.VMEM((128, 128), F32),
            pltpu.VMEM((128, 128), F32),
            dma((11,)),
            dma((2, 8)),
            dma((2, 8)),
            dma((2, 8)),
            dma((2, 8)),
            dma((2, 4)),
            dma((2, 4)),
            dma((4, 8)),
            dma((4, 8)),
            dma((2, 2, 8)),
            dma((2, 2, 8)),
        ],
        compiler_params=pltpu.CompilerParams(
            collective_id=0, has_side_effects=True, vmem_limit_bytes=40 * 1024 * 1024
        ),
        cost_estimate=pl.CostEstimate(
            flops=5_000_000_000, bytes_accessed=8_000_000, transcendentals=40_000
        ),
    )(
        rollout_utterance,
        frame_offset,
        utterance_frames,
        normed_input.reshape(128, 128),
        depth_kernel,
        norm_scale.reshape(1, 128),
        norm_shift.reshape(1, 128),
        frame_cotangent,
        expand_weight.reshape(2048, 128),
        project_weight,
        adapter_weight,
    )
    return stream.reshape(1, 128, 128), normed.reshape(1, 128, 128)


def solution(mesh):
    return jax.shard_map(
        body,
        mesh=mesh,
        in_specs=(
            P("dec", None, "ch"),
            P("dec"),
            P("dec"),
            P("dec"),
            P("dec", None, "ch"),
            P(None, None, "ch"),
            P(None, "ch"),
            P("ch"),
            P("ch"),
            P(),
            P(None, "ch"),
        ),
        out_specs=(P("dec", None, "ch"), P("dec", None, "ch")),
        check_vma=False,
    )
```

```python
import jax
import jax.numpy as jnp
from jax import lax
from jax.experimental import pallas as pl
from jax.experimental.pallas import tpu as pltpu
from jax.sharding import PartitionSpec as P

MESH = pl.DeviceIdType.MESH
F32 = jnp.float32
BF16 = jnp.bfloat16
NY, NX, NCORE, NZ = 4, 4, 2, 8
RING = NX * NCORE


def steps(first, last, work):
    def one(step, carry):
        work(step)
        return carry

    lax.fori_loop(first, last, one, 0)


def rows_of(start, size):
    return pl.ds(pl.multiple_of(start, size), size)


def nt(a, b):
    return lax.dot_general(a, b, (((1,), (1,)), ((), ())), preferred_element_type=F32)


def kernel(
    ids_hbm,
    offs_hbm,
    frames_hbm,
    normed_hbm,
    taps_hbm,
    scale_hbm,
    shift_hbm,
    cot_hbm,
    expand_hbm,
    project_hbm,
    adapter_hbm,
    stream_out,
    normed_out,
    ids_sm,
    offs_sm,
    frames_sm,
    normed_ref,
    taps_ref,
    scale_ref,
    shift_ref,
    cot,
    expand2,
    project,
    adapter,
    fused,
    expand,
    slabs,
    landed,
    ids,
    sel_t,
    sel,
    part,
    part_in,
    fg,
    x_all,
    zsend,
    zrecv,
    owned,
    back,
    pad,
    f_gsw,
    f_val,
    f_gate,
    load_sem,
    s1_send,
    s1_recv,
    id_send,
    id_recv,
    s2_send,
    s2_recv,
    z_send,
    z_recv,
    b_send,
    b_recv,
):
    me = lax.axis_index("dec")
    c = lax.axis_index("ch")
    y = lax.div(me, RING)
    pos_a = lax.rem(me, RING)
    x = lax.div(pos_a, NCORE)
    core = lax.rem(pos_a, NCORE)
    pos_b = y * NCORE + core
    positions = (pos_a, pos_b)

    def group(half, g):
        return lax.rem(g, NCORE) * 8 + half * 4 + lax.div(g, NCORE)

    def ring_dev(half, g):
        if half == 0:
            return y * RING + g
        return lax.div(g, NCORE) * RING + x * NCORE + lax.rem(g, NCORE)

    def line_dev(half, q):
        if half == 0:
            return q * RING + pos_a
        return y * RING + q * NCORE + core

    lines = (y, x)

    small = (
        (offs_hbm, offs_sm),
        (ids_hbm, ids_sm),
        (normed_hbm, normed_ref),
        (frames_hbm, frames_sm),
        (taps_hbm, taps_ref),
        (scale_hbm, scale_ref),
        (shift_hbm, shift_ref),
    )
    pairs = [(cot_hbm.at[r], cot.at[r]) for r in range(8)]
    pairs += [(project_hbm, project), (adapter_hbm, adapter), (expand_hbm, expand2)]
    pairs += small
    loads = [pltpu.make_async_copy(a, b, load_sem.at[n]) for n, (a, b) in enumerate(pairs)]
    for n in (11, 12, 0, 1, 2, 3, 4, 5, 6, 7, 13, 8, 9, 10, 14, 15, 16, 17):
        loads[n].start()

    barrier = pltpu.get_barrier_semaphore()

    def greet(device):
        pl.semaphore_signal(barrier, inc=1, device_id=device, device_id_type=MESH)

    steps(1, RING, lambda o: greet((ring_dev(0, lax.rem(pos_a + o, RING)), c)))
    for other in range(NCORE):
        steps(1, NY, lambda o: greet((ring_dev(1, lax.rem(y + o, NY) * NCORE + other), c)))
    steps(1, NZ, lambda o: greet((me, lax.rem(c + o, NZ))))

    loads[11].wait()
    loads[12].wait()
    row8 = lax.broadcasted_iota(jnp.int32, (8, 128), 0)
    tile = jnp.zeros((8, 128), jnp.int32)
    for r in range(8):
        tile = jnp.where(row8 == r, ids_sm[r], tile)
    ids[0, pos_a] = tile
    ids[1, pos_b] = tile

    srow = lax.broadcasted_iota(jnp.int32, (128, 160), 0)
    scol = lax.broadcasted_iota(jnp.int32, (128, 160), 1)
    diff = scol - srow
    for p in range(4):
        loads[2 * p].wait()
        loads[2 * p + 1].wait()
        sh0 = (diff == offs_sm[2 * p]).astype(F32).astype(BF16)
        sh1 = (diff == offs_sm[2 * p + 1]).astype(F32).astype(BF16)
        for n in range(4):
            cols = slice(n * 256, (n + 1) * 256)
            a = jnp.dot(sh0, cot[2 * p, :, cols], preferred_element_type=F32)
            b = jnp.dot(sh1, cot[2 * p + 1, :, cols], preferred_element_type=F32)
            both = jnp.concatenate([a.reshape(16, 8, 256), b.reshape(16, 8, 256)], axis=1)
            slabs[:, p * 16 : (p + 1) * 16, cols] = both.astype(BF16)

    pl.semaphore_wait(barrier, 20)

    def s1_copy(half, g, slot):
        return pltpu.make_async_remote_copy(
            src_ref=slabs.at[group(half, g)],
            dst_ref=landed.at[half, slot],
            send_sem=s1_send.at[half, g],
            recv_sem=s1_recv.at[half, slot],
            device_id=(ring_dev(half, g), c),
            device_id_type=MESH,
        )

    def id_copy(half, g, slot):
        return pltpu.make_async_remote_copy(
            src_ref=ids.at[half, positions[half]],
            dst_ref=ids.at[half, slot],
            send_sem=id_send.at[half, g],
            recv_sem=id_recv.at[half, slot],
            device_id=(ring_dev(half, g), c),
            device_id_type=MESH,
        )

    def id_start(o):
        for half in range(2):
            g = lax.rem(positions[half] + o, RING)
            id_copy(half, g, positions[half]).start()

    steps(1, RING, id_start)
    for other in range(NCORE):

        def s1_start(o, other=other):
            for half in range(2):
                g = lax.rem(lines[1 - half] + o, 4) * NCORE + other
                s1_copy(half, g, positions[half]).start()

        steps(1, 4, s1_start)

        @pl.when(core != other)
        def _():
            for half in range(2):
                s1_copy(half, lines[1 - half] * NCORE + other, positions[half]).start()


    def z_copy(turn, src, dst, peer, slot):
        return pltpu.make_async_remote_copy(
            src_ref=src,
            dst_ref=dst.at[slot],
            send_sem=z_send.at[turn, peer],
            recv_sem=z_recv.at[turn, slot],
            device_id=(me, peer),
            device_id_type=MESH,
        )

    def x_copy(peer, slot):
        return z_copy(0, normed_ref, x_all, peer, slot)

    loads[13].wait()
    steps(1, NZ, lambda o: x_copy(lax.rem(c + o, NZ), c).start())
    x_all[c] = normed_ref[...]
    for half in range(2):
        landed[half, positions[half]] = slabs[group(half, positions[half])]

    loads[8].wait()
    loads[9].wait()

    def fuse(i):
        mine = rows_of(i * 128, 128)
        for n in range(4):
            cols = slice(n * 256, (n + 1) * 256)
            fused[mine, cols] = jnp.dot(
                project[mine, :], adapter[:, cols], preferred_element_type=F32
            ).astype(BF16)

    steps(0, 8, fuse)

    loads[10].wait()
    for n in range(14, 18):
        loads[n].wait()
    prow = lax.broadcasted_iota(jnp.int32, (256, 256), 0)
    pcol = lax.broadcasted_iota(jnp.int32, (256, 256), 1)
    want = jnp.where(prow < 128, 2 * prow, 2 * prow - 255)
    apart = (pcol == want).astype(F32).astype(BF16)
    for b in range(8):
        both = jnp.dot(apart, expand2[b * 256 : (b + 1) * 256, :], preferred_element_type=F32)
        both = both.astype(BF16)
        expand[b * 128 : (b + 1) * 128, 0:128] = both[:128]
        expand[b * 128 : (b + 1) * 128, 128:256] = both[128:]

    steps(1, NZ, lambda o: x_copy(lax.rem(c + o, NZ), lax.rem(c + o, NZ)).wait_recv())
    both = jnp.zeros((128, 256), F32)
    for b in range(8):
        both += jnp.dot(
            x_all[b], expand[b * 128 : (b + 1) * 128, :], preferred_element_type=F32
        )
    value = both[:, :128]
    sig_gate = jax.nn.sigmoid(both[:, 128:])
    frame = lax.broadcasted_iota(jnp.int32, (128, 128), 0)
    mask = (frame < frames_sm[0]).astype(F32)
    pad[...] = jnp.zeros_like(pad)
    pad[8:136, :] = mask * value * sig_gate
    taps = taps_ref[...].astype(F32)
    depth = jnp.zeros((128, 128), F32)
    for k in range(9):
        depth += taps[k : k + 1, :] * pad[4 + k : 132 + k, :]
    shifted = depth * scale_ref[...] + shift_ref[...]
    sig_shift = jax.nn.sigmoid(shifted)
    f_gsw[...] = sig_shift * (1.0 + shifted * (1.0 - sig_shift)) * scale_ref[...] * mask
    f_val[...] = sig_gate * mask
    f_gate[...] = value * sig_gate * (1.0 - sig_gate) * mask

    lane = lax.broadcasted_iota(jnp.int32, (8, 256), 1)
    same = lax.broadcasted_iota(jnp.int32, (8, 256), 0) == lax.rem(lane, 8)
    unit = lax.div(lane, 8)
    turned = (lax.rem(lax.div(unit, 2), 4) * NX + lax.div(unit, 8)) * NCORE + lax.rem(unit, 2)
    utts = (unit, turned)
    for half in range(2):

        def id_wait(o, half=half):
            slot = lax.rem(positions[half] + o, RING)
            id_copy(half, slot, slot).wait_recv()

        steps(1, RING, id_wait)

        def choose(s, half=half):
            for r in range(8):
                row = ids[half, s, r : r + 1, :]
                wide = jnp.concatenate([row, row], axis=1)
                hit = jnp.logical_and(same, wide == utts[half])
                sel_t[rows_of(s * 64 + r * 8, 8), :] = hit.astype(F32)

        steps(0, 8, choose)
        sel[half] = sel_t[...].T.astype(BF16)

    def s2_copy(half, q, slot):
        return pltpu.make_async_remote_copy(
            src_ref=part.at[half, q],
            dst_ref=part_in.at[half, slot],
            send_sem=s2_send.at[half, q],
            recv_sem=s2_recv.at[half, slot],
            device_id=(line_dev(half, q), c),
            device_id_type=MESH,
        )

    for half in range(2):

        def s1_wait(o, half=half):
            slot = lax.rem(positions[half] + o, RING)
            s1_copy(half, slot, slot).wait_recv()

        steps(1, RING, s1_wait)
        for n in range(4):
            cols = slice(n * 256, (n + 1) * 256)
            got = jnp.dot(
                sel[half],
                landed[half, :, :, cols].reshape(512, 256),
                preferred_element_type=F32,
            )
            part[half, :, :, cols] = got.astype(BF16).reshape(4, 64, 256)

        def s2_start(o, half=half):
            s2_copy(half, lax.rem(lines[half] + o, 4), lines[half]).start()

        steps(1, 4, s2_start)
        part_in[half, lines[half]] = part[half, lines[half]]

    for half in range(2):

        def s2_wait(o, half=half):
            slot = lax.rem(lines[half] + o, 4)
            s2_copy(half, slot, slot).wait_recv()

        steps(1, 4, s2_wait)
        total = part_in[half, 0].astype(F32)
        for q in range(1, 4):
            total += part_in[half, q].astype(F32)
        fg[half * 64 : (half + 1) * 64, :] = total.astype(BF16)

    for kind, weight in ((0, fused), (1, adapter)):
        for n in range(4):
            got = nt(fg[...], weight[n * 256 : (n + 1) * 256, :]).astype(BF16)
            zsend[kind, 2 * n] = got[:, :128]
            zsend[kind, 2 * n + 1] = got[:, 128:]

        def zk_start(o, kind=kind):
            peer = lax.rem(c + o, NZ)
            z_copy(1 + kind, zsend.at[kind, peer], zrecv.at[kind], peer, c).start()

        steps(1, NZ, zk_start)
        zrecv[kind, c] = zsend[kind, c]

    def back_copy(kind, half, g, slot):
        return pltpu.make_async_remote_copy(
            src_ref=owned.at[kind, rows_of(half * 64 + g * 8, 8), :],
            dst_ref=back.at[kind, rows_of(group(half, slot) * 8, 8), :],
            send_sem=b_send.at[kind, half, g],
            recv_sem=b_recv.at[kind, half, slot],
            device_id=(ring_dev(half, g), c),
            device_id_type=MESH,
        )

    def z_sum(kind):
        def zk_wait(o):
            slot = lax.rem(c + o, NZ)
            z_copy(1 + kind, zsend.at[kind, slot], zrecv.at[kind], slot, slot).wait_recv()

        steps(1, NZ, zk_wait)
        total = zrecv[kind, 0].astype(F32)
        for b in range(1, NZ):
            total += zrecv[kind, b].astype(F32)
        return total

    def give_back(kind):
        owned[kind] = z_sum(kind)

        def go(o):
            for half in range(2):
                back_copy(kind, half, lax.rem(positions[half] + o, RING), positions[half]).start()

        steps(1, RING, go)
        for half in range(2):
            mine = rows_of(half * 64 + positions[half] * 8, 8)
            home = rows_of(group(half, positions[half]) * 8, 8)
            back[kind, home, :] = owned[kind, mine, :]

    def back_wait(kind):
        def hold(o):
            for half in range(2):
                slot = lax.rem(positions[half] + o, RING)
                back_copy(kind, half, slot, slot).wait_recv()

        steps(1, RING, hold)

    give_back(0)
    back_wait(0)
    pad[8:136, :] = back[0] * f_gsw[...]
    grad_glu = jnp.zeros((128, 128), F32)
    for k in range(9):
        grad_glu += taps[k : k + 1, :] * pad[12 - k : 140 - k, :]
    grad_expanded = jnp.concatenate(
        [grad_glu * f_val[...], grad_glu * f_gate[...]], axis=1
    ).astype(BF16)
    for n in range(4):
        got = nt(grad_expanded, expand[n * 256 : (n + 1) * 256, :]).astype(BF16)
        zsend[2, 2 * n] = got[:, :128]
        zsend[2, 2 * n + 1] = got[:, 128:]

    def z2_start(o):
        peer = lax.rem(c + o, NZ)
        z_copy(3, zsend.at[2, peer], zrecv.at[2], peer, c).start()

    steps(1, NZ, z2_start)
    zrecv[2, c] = zsend[2, c]

    give_back(1)
    back_wait(1)
    stream_out[...] = (back[1] * mask).astype(BF16)
    normed_out[...] = z_sum(2).astype(BF16)

    def sent(o):
        peer = lax.rem(c + o, NZ)
        x_copy(peer, c).wait_send()
        for kind in range(3):
            z_copy(1 + kind, zsend.at[kind, peer], zrecv.at[kind], peer, c).wait_send()
        for half in range(2):
            g = lax.rem(positions[half] + o, RING)
            s1_copy(half, g, positions[half]).wait_send()
            id_copy(half, g, positions[half]).wait_send()
            for kind in range(2):
                back_copy(kind, half, g, positions[half]).wait_send()

    steps(1, NZ, sent)

    def sent_line(o):
        for half in range(2):
            s2_copy(half, lax.rem(lines[half] + o, 4), lines[half]).wait_send()

    steps(1, 4, sent_line)


def body(
    frame_cotangent,
    rollout_utterance,
    frame_offset,
    utterance_frames,
    normed_input,
    expand_weight,
    depth_kernel,
    norm_scale,
    norm_shift,
    project_weight,
    adapter_weight,
):
    vmem = pl.BlockSpec(memory_space=pltpu.VMEM)
    hbm = pl.BlockSpec(memory_space=pl.ANY)
    dma = pltpu.SemaphoreType.DMA
    block = jax.ShapeDtypeStruct((128, 128), BF16)
    stream, normed = pl.pallas_call(
        kernel,
        out_shape=(block, block),
        in_specs=[hbm] * 11,
        out_specs=(vmem, vmem),
        scratch_shapes=[
            pltpu.SMEM((8,), jnp.int32),
            pltpu.SMEM((8,), jnp.int32),
            pltpu.SMEM((1,), jnp.int32),
            pltpu.VMEM((128, 128), BF16),
            pltpu.VMEM((9, 128), BF16),
            pltpu.VMEM((1, 128), F32),
            pltpu.VMEM((1, 128), F32),
            pltpu.VMEM((8, 160, 1024), BF16),
            pltpu.VMEM((2048, 128), BF16),
            pltpu.VMEM((1024, 1024), BF16),
            pltpu.VMEM((1024, 1024), BF16),
            pltpu.VMEM((1024, 1024), BF16),
            pltpu.VMEM((1024, 256), BF16),
            pltpu.VMEM((16, 64, 1024), BF16),
            pltpu.VMEM((2, 8, 64, 1024), BF16),
            pltpu.VMEM((2, 8, 8, 128), jnp.int32),
            pltpu.VMEM((512, 256), F32),
            pltpu.VMEM((2, 256, 512), BF16),
            pltpu.VMEM((2, 4, 64, 1024), BF16),
            pltpu.VMEM((2, 4, 64, 1024), BF16),
            pltpu.VMEM((128, 1024), BF16),
            pltpu.VMEM((8, 128, 128), BF16),
            pltpu.VMEM((3, 8, 128, 128), BF16),
            pltpu.VMEM((3, 8, 128, 128), BF16),
            pltpu.VMEM((2, 128, 128), F32),
            pltpu.VMEM((2, 128, 128), F32),
            pltpu.VMEM((144, 128), F32),
            pltpu.VMEM((128, 128), F32),
            pltpu.VMEM((128, 128), F32),
            pltpu.VMEM((128, 128), F32),
            dma((18,)),
            dma((2, 8)),
            dma((2, 8)),
            dma((2, 8)),
            dma((2, 8)),
            dma((2, 4)),
            dma((2, 4)),
            dma((4, 8)),
            dma((4, 8)),
            dma((2, 2, 8)),
            dma((2, 2, 8)),
        ],
        compiler_params=pltpu.CompilerParams(
            collective_id=0, has_side_effects=True, vmem_limit_bytes=63 * 1024 * 1024
        ),
        cost_estimate=pl.CostEstimate(
            flops=5_000_000_000, bytes_accessed=8_000_000, transcendentals=40_000
        ),
    )(
        rollout_utterance,
        frame_offset,
        utterance_frames,
        normed_input.reshape(128, 128),
        depth_kernel,
        norm_scale.reshape(1, 128),
        norm_shift.reshape(1, 128),
        frame_cotangent,
        expand_weight.reshape(2048, 128),
        project_weight,
        adapter_weight,
    )
    return stream.reshape(1, 128, 128), normed.reshape(1, 128, 128)


def solution(mesh):
    return jax.shard_map(
        body,
        mesh=mesh,
        in_specs=(
            P("dec", None, "ch"),
            P("dec"),
            P("dec"),
            P("dec"),
            P("dec", None, "ch"),
            P(None, None, "ch"),
            P(None, "ch"),
            P("ch"),
            P("ch"),
            P(),
            P(None, "ch"),
        ),
        out_specs=(P("dec", None, "ch"), P("dec", None, "ch")),
        check_vma=False,
    )
```

```python
import jax
import jax.numpy as jnp
from jax import lax
from jax.experimental import pallas as pl
from jax.experimental.pallas import tpu as pltpu
from jax.sharding import PartitionSpec as P

MESH = pl.DeviceIdType.MESH
F32 = jnp.float32
BF16 = jnp.bfloat16
NY, NX, NCORE, NZ = 4, 4, 2, 8
RING = NX * NCORE


def steps(first, last, work):
    def one(step, carry):
        work(step)
        return carry

    lax.fori_loop(first, last, one, 0)


def rows_of(start, size):
    return pl.ds(pl.multiple_of(start, size), size)


def nt(a, b):
    return lax.dot_general(a, b, (((1,), (1,)), ((), ())), preferred_element_type=F32)


def kernel(
    ids_hbm,
    offs_hbm,
    frames_hbm,
    normed_hbm,
    taps_hbm,
    scale_hbm,
    shift_hbm,
    cot_hbm,
    expand_hbm,
    project_hbm,
    adapter_hbm,
    stream_out,
    normed_out,
    ids_sm,
    offs_sm,
    frames_sm,
    normed_ref,
    taps_ref,
    scale_ref,
    shift_ref,
    cot,
    expand2,
    project,
    adapter,
    fused,
    expand,
    slabs,
    landed,
    ids,
    sel_t,
    sel,
    part,
    part_in,
    fg,
    x_all,
    zsend,
    zrecv,
    wsend,
    wrecv,
    fsend,
    frecv,
    owned,
    back,
    pad,
    f_gsw,
    f_val,
    f_gate,
    load_sem,
    s1_send,
    s1_recv,
    id_send,
    id_recv,
    s2_send,
    s2_recv,
    z_send,
    z_recv,
    b_send,
    b_recv,
):
    me = lax.axis_index("dec")
    c = lax.axis_index("ch")
    y = lax.div(me, RING)
    pos_a = lax.rem(me, RING)
    x = lax.div(pos_a, NCORE)
    core = lax.rem(pos_a, NCORE)
    pos_b = y * NCORE + core
    positions = (pos_a, pos_b)

    def group(half, g):
        return lax.rem(g, NCORE) * 8 + half * 4 + lax.div(g, NCORE)

    def ring_dev(half, g):
        if half == 0:
            return y * RING + g
        return lax.div(g, NCORE) * RING + x * NCORE + lax.rem(g, NCORE)

    def line_dev(half, q):
        if half == 0:
            return q * RING + pos_a
        return y * RING + q * NCORE + core

    lines = (y, x)

    small = (
        (offs_hbm, offs_sm),
        (ids_hbm, ids_sm),
        (normed_hbm, normed_ref),
        (frames_hbm, frames_sm),
        (taps_hbm, taps_ref),
        (scale_hbm, scale_ref),
        (shift_hbm, shift_ref),
    )
    pairs = [(cot_hbm.at[r], cot.at[r]) for r in range(8)]
    pairs += [(project_hbm, project), (adapter_hbm, adapter), (expand_hbm, expand2)]
    pairs += small
    loads = [pltpu.make_async_copy(a, b, load_sem.at[n]) for n, (a, b) in enumerate(pairs)]
    for n in (11, 12, 0, 1, 2, 3, 4, 5, 6, 7, 13, 8, 9, 10, 14, 15, 16, 17):
        loads[n].start()

    barrier = pltpu.get_barrier_semaphore()

    def greet(device):
        pl.semaphore_signal(barrier, inc=1, device_id=device, device_id_type=MESH)

    steps(1, RING, lambda o: greet((ring_dev(0, lax.rem(pos_a + o, RING)), c)))
    for other in range(NCORE):
        steps(1, NY, lambda o: greet((ring_dev(1, lax.rem(y + o, NY) * NCORE + other), c)))
    steps(1, NZ, lambda o: greet((me, lax.rem(c + o, NZ))))

    loads[11].wait()
    loads[12].wait()
    row8 = lax.broadcasted_iota(jnp.int32, (8, 128), 0)
    tile = jnp.zeros((8, 128), jnp.int32)
    for r in range(8):
        tile = jnp.where(row8 == r, ids_sm[r], tile)
    ids[0, pos_a] = tile
    ids[1, pos_b] = tile

    srow = lax.broadcasted_iota(jnp.int32, (128, 160), 0)
    scol = lax.broadcasted_iota(jnp.int32, (128, 160), 1)
    diff = scol - srow
    for p in range(4):
        loads[2 * p].wait()
        loads[2 * p + 1].wait()
        sh0 = (diff == offs_sm[2 * p]).astype(F32).astype(BF16)
        sh1 = (diff == offs_sm[2 * p + 1]).astype(F32).astype(BF16)
        for n in range(4):
            cols = slice(n * 256, (n + 1) * 256)
            a = jnp.dot(sh0, cot[2 * p, :, cols], preferred_element_type=F32)
            b = jnp.dot(sh1, cot[2 * p + 1, :, cols], preferred_element_type=F32)
            both = jnp.concatenate([a.reshape(16, 8, 256), b.reshape(16, 8, 256)], axis=1)
            slabs[:, p * 16 : (p + 1) * 16, cols] = both.astype(BF16)

    pl.semaphore_wait(barrier, 20)

    def s1_copy(half, g, slot):
        return pltpu.make_async_remote_copy(
            src_ref=slabs.at[group(half, g)],
            dst_ref=landed.at[half, slot],
            send_sem=s1_send.at[half, g],
            recv_sem=s1_recv.at[half, slot],
            device_id=(ring_dev(half, g), c),
            device_id_type=MESH,
        )

    def id_copy(half, g, slot):
        return pltpu.make_async_remote_copy(
            src_ref=ids.at[half, positions[half]],
            dst_ref=ids.at[half, slot],
            send_sem=id_send.at[half, g],
            recv_sem=id_recv.at[half, slot],
            device_id=(ring_dev(half, g), c),
            device_id_type=MESH,
        )

    def id_start(o):
        for half in range(2):
            g = lax.rem(positions[half] + o, RING)
            id_copy(half, g, positions[half]).start()

    steps(1, RING, id_start)
    for other in range(NCORE):

        def s1_start(o, other=other):
            for half in range(2):
                g = lax.rem(lines[1 - half] + o, 4) * NCORE + other
                s1_copy(half, g, positions[half]).start()

        steps(1, 4, s1_start)

        @pl.when(core != other)
        def _():
            for half in range(2):
                s1_copy(half, lines[1 - half] * NCORE + other, positions[half]).start()


    def z_copy(turn, src, dst, peer, slot):
        return pltpu.make_async_remote_copy(
            src_ref=src,
            dst_ref=dst.at[slot],
            send_sem=z_send.at[turn, peer],
            recv_sem=z_recv.at[turn, slot],
            device_id=(me, peer),
            device_id_type=MESH,
        )

    def x_copy(peer, slot):
        return z_copy(0, normed_ref, x_all, peer, slot)

    loads[13].wait()
    steps(1, NZ, lambda o: x_copy(lax.rem(c + o, NZ), c).start())
    x_all[c] = normed_ref[...]
    for half in range(2):
        landed[half, positions[half]] = slabs[group(half, positions[half])]

    loads[8].wait()
    loads[9].wait()

    def fuse(i):
        mine = rows_of(i * 128, 128)
        for n in range(4):
            cols = slice(n * 256, (n + 1) * 256)
            fused[mine, cols] = jnp.dot(
                project[mine, :], adapter[:, cols], preferred_element_type=F32
            ).astype(BF16)

    steps(0, 8, fuse)

    loads[10].wait()
    for n in range(14, 18):
        loads[n].wait()
    prow = lax.broadcasted_iota(jnp.int32, (256, 256), 0)
    pcol = lax.broadcasted_iota(jnp.int32, (256, 256), 1)
    want = jnp.where(prow < 128, 2 * prow, 2 * prow - 255)
    apart = (pcol == want).astype(F32).astype(BF16)
    for b in range(8):
        both = jnp.dot(apart, expand2[b * 256 : (b + 1) * 256, :], preferred_element_type=F32)
        both = both.astype(BF16)
        expand[b * 128 : (b + 1) * 128, 0:128] = both[:128]
        expand[b * 128 : (b + 1) * 128, 128:256] = both[128:]

    steps(1, NZ, lambda o: x_copy(lax.rem(c + o, NZ), lax.rem(c + o, NZ)).wait_recv())
    both = jnp.zeros((128, 256), F32)
    for b in range(8):
        both += jnp.dot(
            x_all[b], expand[b * 128 : (b + 1) * 128, :], preferred_element_type=F32
        )
    value = both[:, :128]
    sig_gate = jax.nn.sigmoid(both[:, 128:])
    frame = lax.broadcasted_iota(jnp.int32, (128, 128), 0)
    mask = (frame < frames_sm[0]).astype(F32)
    pad[...] = jnp.zeros_like(pad)
    pad[8:136, :] = mask * value * sig_gate
    taps = taps_ref[...].astype(F32)
    depth = jnp.zeros((128, 128), F32)
    for k in range(9):
        depth += taps[k : k + 1, :] * pad[4 + k : 132 + k, :]
    shifted = depth * scale_ref[...] + shift_ref[...]
    sig_shift = jax.nn.sigmoid(shifted)
    f_gsw[...] = sig_shift * (1.0 + shifted * (1.0 - sig_shift)) * scale_ref[...] * mask
    f_val[...] = sig_gate * mask
    f_gate[...] = value * sig_gate * (1.0 - sig_gate) * mask

    lane = lax.broadcasted_iota(jnp.int32, (8, 256), 1)
    same = lax.broadcasted_iota(jnp.int32, (8, 256), 0) == lax.rem(lane, 8)
    unit = lax.div(lane, 8)
    outer = lax.div(unit, 8)
    inner = lax.rem(unit, 4)
    odd = lax.rem(lax.div(unit, 4), NCORE)
    utts = ((outer * NX + inner) * NCORE + odd, (inner * NX + outer) * NCORE + odd)
    for half in range(2):

        def id_wait(o, half=half):
            slot = lax.rem(positions[half] + o, RING)
            id_copy(half, slot, slot).wait_recv()

        steps(1, RING, id_wait)

        def choose(s, half=half):
            for r in range(8):
                row = ids[half, s, r : r + 1, :]
                wide = jnp.concatenate([row, row], axis=1)
                hit = jnp.logical_and(same, wide == utts[half])
                sel_t[rows_of(s * 64 + r * 8, 8), :] = hit.astype(F32)

        steps(0, 8, choose)
        sel[half] = sel_t[...].T.astype(BF16)

    def s2_copy(half, to, q, slot):
        return pltpu.make_async_remote_copy(
            src_ref=part.at[half, q, to],
            dst_ref=part_in.at[half, to, slot],
            send_sem=s2_send.at[half, to, q],
            recv_sem=s2_recv.at[half, to, slot],
            device_id=(line_dev(half, q), c),
            device_id_type=MESH,
        )

    for half in range(2):

        def s1_wait(o, half=half):
            slot = lax.rem(positions[half] + o, RING)
            s1_copy(half, slot, slot).wait_recv()

        steps(1, RING, s1_wait)
        for n in range(4):
            cols = slice(n * 256, (n + 1) * 256)
            got = jnp.dot(
                sel[half],
                landed[half, :, :, cols].reshape(512, 256),
                preferred_element_type=F32,
            )
            part[half, :, :, :, cols] = got.astype(BF16).reshape(4, 2, 32, 256)

        def s2_start(o, half=half):
            s2_copy(half, 0, lax.rem(lines[half] + o, 4), lines[half]).start()

        steps(1, 4, s2_start)
        for to in range(2):
            part_in[half, to, lines[half]] = part[half, lines[half], to]

    def s2_start(o):
        for half in range(2):
            s2_copy(half, 1, lax.rem(lines[half] + o, 4), lines[half]).start()

    steps(1, 4, s2_start)

    def z_part(to, peer, slot):
        return z_copy(1 + to, zsend.at[to, peer], zrecv.at[to], peer, slot)

    def z_stream(peer, slot):
        return z_copy(3, wsend.at[peer], wrecv, peer, slot)

    for to in range(2):
        for half in range(2):

            def s2_wait(o, half=half, to=to):
                slot = lax.rem(lines[half] + o, 4)
                s2_copy(half, to, slot, slot).wait_recv()

            steps(1, 4, s2_wait)
            total = part_in[half, to, 0].astype(F32)
            for q in range(1, 4):
                total += part_in[half, to, q].astype(F32)
            fg[to * 64 + half * 32 : to * 64 + half * 32 + 32, :] = total.astype(BF16)
        for n in range(4):
            got = nt(fg[to * 64 : to * 64 + 64, :], fused[n * 256 : (n + 1) * 256, :])
            got = got.astype(BF16)
            zsend[to, 2 * n] = got[:, :128]
            zsend[to, 2 * n + 1] = got[:, 128:]

        def part_start(o, to=to):
            z_part(to, lax.rem(c + o, NZ), c).start()

        steps(1, NZ, part_start)
        zrecv[to, c] = zsend[to, c]

    for n in range(4):
        got = nt(fg[...], adapter[n * 256 : (n + 1) * 256, :]).astype(BF16)
        wsend[2 * n] = got[:, :128]
        wsend[2 * n + 1] = got[:, 128:]
    steps(1, NZ, lambda o: z_stream(lax.rem(c + o, NZ), c).start())
    wrecv[c] = wsend[c]

    def z_sum(copy, into):
        def hold(o):
            slot = lax.rem(c + o, NZ)
            copy(slot, slot).wait_recv()

        steps(1, NZ, hold)
        total = into[0].astype(F32)
        for b in range(1, NZ):
            total += into[b].astype(F32)
        return total

    def back_copy(kind, half, to, q, slot):
        if half == 0:
            device = y * RING + q * NCORE + to
        else:
            device = q * RING + x * NCORE + to
        return pltpu.make_async_remote_copy(
            src_ref=owned.at[kind, rows_of(to * 64 + half * 32 + q * 8, 8), :],
            dst_ref=back.at[kind, rows_of(group(half, slot) * 8, 8), :],
            send_sem=b_send.at[kind, half, to * 4 + q],
            recv_sem=b_recv.at[kind, half, slot],
            device_id=(device, c),
            device_id_type=MESH,
        )

    def give_back(kind, to):
        def go(o):
            for half in range(2):
                q = lax.rem(lines[1 - half] + o, 4)
                back_copy(kind, half, to, q, positions[half]).start()

        steps(1, 4, go)

        @pl.when(core != to)
        def _():
            for half in range(2):
                back_copy(kind, half, to, lines[1 - half], positions[half]).start()

        @pl.when(core == to)
        def _():
            for half in range(2):
                mine = rows_of(to * 64 + half * 32 + lines[1 - half] * 8, 8)
                home = rows_of(group(half, positions[half]) * 8, 8)
                back[kind, home, :] = owned[kind, mine, :]

    def back_wait(kind, other):
        def hold(o):
            for half in range(2):
                slot = lax.rem(lines[1 - half] + o, 4) * NCORE + other
                back_copy(kind, half, 0, 0, slot).wait_recv()

        steps(1, 4, hold)

        @pl.when(core != other)
        def _():
            for half in range(2):
                back_copy(kind, half, 0, 0, lines[1 - half] * NCORE + other).wait_recv()

    def last_copy(turn, peer, slot):
        rows = slice(0, 48) if turn == 0 else slice(48, 128)
        return pltpu.make_async_remote_copy(
            src_ref=fsend.at[peer, rows, :],
            dst_ref=frecv.at[slot, rows, :],
            send_sem=z_send.at[4 + turn, peer],
            recv_sem=z_recv.at[4 + turn, slot],
            device_id=(me, peer),
            device_id_type=MESH,
        )

    def last_part(turn):
        lo, hi = (0, 48) if turn == 0 else (48, 128)
        new = slice(turn * 64, turn * 64 + 64)
        pad[8 + turn * 64 : 72 + turn * 64, :] = back[0, new, :] * f_gsw[new, :]
        grad_glu = jnp.zeros((hi - lo, 128), F32)
        for k in range(9):
            grad_glu += taps[k : k + 1, :] * pad[12 - k + lo : 12 - k + hi, :]
        grad_expanded = jnp.concatenate(
            [grad_glu * f_val[lo:hi, :], grad_glu * f_gate[lo:hi, :]], axis=1
        ).astype(BF16)
        for n in range(4):
            got = nt(grad_expanded, expand[n * 256 : (n + 1) * 256, :]).astype(BF16)
            fsend[2 * n, lo:hi, :] = got[:, :128]
            fsend[2 * n + 1, lo:hi, :] = got[:, 128:]
        steps(1, NZ, lambda o: last_copy(turn, lax.rem(c + o, NZ), c).start())

    def early():
        back_wait(0, 0)
        last_part(0)

    pl.when(core == 1)(early)
    for to in range(2):
        owned[0, to * 64 : to * 64 + 64, :] = z_sum(
            lambda peer, slot, to=to: z_part(to, peer, slot), zrecv.at[to]
        )
        give_back(0, to)
    pl.when(core == 0)(early)
    back_wait(0, 1)
    last_part(1)
    frecv[c] = fsend[c]

    owned[1] = z_sum(z_stream, wrecv)
    for to in range(2):
        give_back(1, to)
    for other in range(2):
        back_wait(1, other)
    stream_out[...] = back[1] * mask

    def last_wait(o):
        slot = lax.rem(c + o, NZ)
        for turn in range(2):
            last_copy(turn, slot, slot).wait_recv()

    steps(1, NZ, last_wait)
    total = frecv[0].astype(F32)
    for b in range(1, NZ):
        total += frecv[b].astype(F32)
    normed_out[...] = total

    def sent(o):
        peer = lax.rem(c + o, NZ)
        x_copy(peer, c).wait_send()
        z_stream(peer, c).wait_send()
        for turn in range(2):
            z_part(turn, peer, c).wait_send()
            last_copy(turn, peer, c).wait_send()
        for half in range(2):
            g = lax.rem(positions[half] + o, RING)
            s1_copy(half, g, positions[half]).wait_send()
            id_copy(half, g, positions[half]).wait_send()

    steps(1, NZ, sent)

    def sent_line(o):
        for half in range(2):
            for to in range(2):
                s2_copy(half, to, lax.rem(lines[half] + o, 4), lines[half]).wait_send()
                q = lax.rem(lines[1 - half] + o, 4)
                for kind in range(2):
                    back_copy(kind, half, to, q, positions[half]).wait_send()

    steps(1, 4, sent_line)
    for to in range(2):

        @pl.when(core != to)
        def _():
            for half in range(2):
                for kind in range(2):
                    back_copy(kind, half, to, lines[1 - half], positions[half]).wait_send()


def body(
    frame_cotangent,
    rollout_utterance,
    frame_offset,
    utterance_frames,
    normed_input,
    expand_weight,
    depth_kernel,
    norm_scale,
    norm_shift,
    project_weight,
    adapter_weight,
):
    vmem = pl.BlockSpec(memory_space=pltpu.VMEM)
    hbm = pl.BlockSpec(memory_space=pl.ANY)
    dma = pltpu.SemaphoreType.DMA
    block = jax.ShapeDtypeStruct((128, 128), F32)
    stream, normed = pl.pallas_call(
        kernel,
        out_shape=(block, block),
        in_specs=[hbm] * 11,
        out_specs=(vmem, vmem),
        scratch_shapes=[
            pltpu.SMEM((8,), jnp.int32),
            pltpu.SMEM((8,), jnp.int32),
            pltpu.SMEM((1,), jnp.int32),
            pltpu.VMEM((128, 128), BF16),
            pltpu.VMEM((9, 128), BF16),
            pltpu.VMEM((1, 128), F32),
            pltpu.VMEM((1, 128), F32),
            pltpu.VMEM((8, 160, 1024), BF16),
            pltpu.VMEM((2048, 128), BF16),
            pltpu.VMEM((1024, 1024), BF16),
            pltpu.VMEM((1024, 1024), BF16),
            pltpu.VMEM((1024, 1024), BF16),
            pltpu.VMEM((1024, 256), BF16),
            pltpu.VMEM((16, 64, 1024), BF16),
            pltpu.VMEM((2, 8, 64, 1024), BF16),
            pltpu.VMEM((2, 8, 8, 128), jnp.int32),
            pltpu.VMEM((512, 256), F32),
            pltpu.VMEM((2, 256, 512), BF16),
            pltpu.VMEM((2, 4, 2, 32, 1024), BF16),
            pltpu.VMEM((2, 2, 4, 32, 1024), BF16),
            pltpu.VMEM((128, 1024), BF16),
            pltpu.VMEM((8, 128, 128), BF16),
            pltpu.VMEM((2, 8, 64, 128), BF16),
            pltpu.VMEM((2, 8, 64, 128), BF16),
            pltpu.VMEM((8, 128, 128), BF16),
            pltpu.VMEM((8, 128, 128), BF16),
            pltpu.VMEM((8, 128, 128), BF16),
            pltpu.VMEM((8, 128, 128), BF16),
            pltpu.VMEM((2, 128, 128), F32),
            pltpu.VMEM((2, 128, 128), F32),
            pltpu.VMEM((144, 128), F32),
            pltpu.VMEM((128, 128), F32),
            pltpu.VMEM((128, 128), F32),
            pltpu.VMEM((128, 128), F32),
            dma((18,)),
            dma((2, 8)),
            dma((2, 8)),
            dma((2, 8)),
            dma((2, 8)),
            dma((2, 2, 4)),
            dma((2, 2, 4)),
            dma((6, 8)),
            dma((6, 8)),
            dma((2, 2, 8)),
            dma((2, 2, 8)),
        ],
        compiler_params=pltpu.CompilerParams(
            collective_id=0, has_side_effects=True, vmem_limit_bytes=63 * 1024 * 1024
        ),
        cost_estimate=pl.CostEstimate(
            flops=5_000_000_000, bytes_accessed=8_000_000, transcendentals=40_000
        ),
    )(
        rollout_utterance,
        frame_offset,
        utterance_frames,
        normed_input.reshape(128, 128),
        depth_kernel,
        norm_scale.reshape(1, 128),
        norm_shift.reshape(1, 128),
        frame_cotangent,
        expand_weight.reshape(2048, 128),
        project_weight,
        adapter_weight,
    )
    stream, normed = lax.optimization_barrier((stream, normed))
    return stream.reshape(1, 128, 128).astype(BF16), normed.reshape(1, 128, 128).astype(BF16)


def solution(mesh):
    return jax.shard_map(
        body,
        mesh=mesh,
        in_specs=(
            P("dec", None, "ch"),
            P("dec"),
            P("dec"),
            P("dec"),
            P("dec", None, "ch"),
            P(None, None, "ch"),
            P(None, "ch"),
            P("ch"),
            P("ch"),
            P(),
            P(None, "ch"),
        ),
        out_specs=(P("dec", None, "ch"), P("dec", None, "ch")),
        check_vma=False,
    )
```

```python
import jax
import jax.numpy as jnp
from jax import lax
from jax.experimental import pallas as pl
from jax.experimental.pallas import tpu as pltpu
from jax.sharding import PartitionSpec as P

MESH = pl.DeviceIdType.MESH
F32 = jnp.float32
BF16 = jnp.bfloat16
NY, NX, NCORE, NZ = 4, 4, 2, 8
FAR_FIRST = (4, 3, 5, 2, 6, 1, 7)
RING = NX * NCORE


def steps(first, last, work):
    def one(step, carry):
        work(step)
        return carry

    lax.fori_loop(first, last, one, 0)


def rows_of(start, size):
    return pl.ds(pl.multiple_of(start, size), size)


def nt(a, b):
    return lax.dot_general(a, b, (((1,), (1,)), ((), ())), preferred_element_type=F32)


def kernel(
    ids_hbm,
    offs_hbm,
    frames_hbm,
    normed_hbm,
    taps_hbm,
    scale_hbm,
    shift_hbm,
    cot_hbm,
    expand_hbm,
    project_hbm,
    adapter_hbm,
    stream_out,
    normed_out,
    ids_sm,
    offs_sm,
    frames_sm,
    normed_ref,
    taps_ref,
    scale_ref,
    shift_ref,
    cot,
    expand2,
    project,
    adapter,
    fused,
    expand,
    slabs,
    landed,
    ids,
    sel_t,
    sel,
    part,
    part_in,
    fg,
    x_all,
    zsend,
    zrecv,
    wsend,
    wrecv,
    fsend,
    frecv,
    owned,
    back,
    pad,
    f_gsw,
    f_val,
    f_gate,
    load_sem,
    s1_send,
    s1_recv,
    id_send,
    id_recv,
    s2_send,
    s2_recv,
    z_send,
    z_recv,
    b_send,
    b_recv,
):
    me = lax.axis_index("dec")
    c = lax.axis_index("ch")
    y = lax.div(me, RING)
    pos_a = lax.rem(me, RING)
    x = lax.div(pos_a, NCORE)
    core = lax.rem(pos_a, NCORE)
    pos_b = y * NCORE + core
    positions = (pos_a, pos_b)

    def group(half, g):
        return lax.rem(g, NCORE) * 8 + half * 4 + lax.div(g, NCORE)

    def ring_dev(half, g):
        if half == 0:
            return y * RING + g
        return lax.div(g, NCORE) * RING + x * NCORE + lax.rem(g, NCORE)

    def line_dev(half, q):
        if half == 0:
            return q * RING + pos_a
        return y * RING + q * NCORE + core

    lines = (y, x)

    small = (
        (offs_hbm, offs_sm),
        (ids_hbm, ids_sm),
        (normed_hbm, normed_ref),
        (frames_hbm, frames_sm),
        (taps_hbm, taps_ref),
        (scale_hbm, scale_ref),
        (shift_hbm, shift_ref),
    )
    pairs = [(cot_hbm.at[r], cot.at[r]) for r in range(8)]
    pairs += [(project_hbm, project), (adapter_hbm, adapter), (expand_hbm, expand2)]
    pairs += small
    loads = [pltpu.make_async_copy(a, b, load_sem.at[n]) for n, (a, b) in enumerate(pairs)]
    for n in (11, 12, 0, 1, 2, 3, 4, 5, 6, 7, 13, 8, 9, 10, 14, 15, 16, 17):
        loads[n].start()

    barrier = pltpu.get_barrier_semaphore()

    def greet(device):
        pl.semaphore_signal(barrier, inc=1, device_id=device, device_id_type=MESH)

    steps(1, RING, lambda o: greet((ring_dev(0, lax.rem(pos_a + o, RING)), c)))
    for other in range(NCORE):
        steps(1, NY, lambda o: greet((ring_dev(1, lax.rem(y + o, NY) * NCORE + other), c)))
    steps(1, NZ, lambda o: greet((me, lax.rem(c + o, NZ))))

    loads[11].wait()
    loads[12].wait()
    row8 = lax.broadcasted_iota(jnp.int32, (8, 128), 0)
    tile = jnp.zeros((8, 128), jnp.int32)
    for r in range(8):
        tile = jnp.where(row8 == r, ids_sm[r], tile)
    ids[0, pos_a] = tile
    ids[1, pos_b] = tile

    srow = lax.broadcasted_iota(jnp.int32, (128, 160), 0)
    scol = lax.broadcasted_iota(jnp.int32, (128, 160), 1)
    diff = scol - srow
    for p in range(4):
        loads[2 * p].wait()
        loads[2 * p + 1].wait()
        sh0 = (diff == offs_sm[2 * p]).astype(F32).astype(BF16)
        sh1 = (diff == offs_sm[2 * p + 1]).astype(F32).astype(BF16)
        for n in range(4):
            cols = slice(n * 256, (n + 1) * 256)
            a = jnp.dot(sh0, cot[2 * p, :, cols], preferred_element_type=F32)
            b = jnp.dot(sh1, cot[2 * p + 1, :, cols], preferred_element_type=F32)
            both = jnp.concatenate([a.reshape(16, 8, 256), b.reshape(16, 8, 256)], axis=1)
            slabs[:, p * 16 : (p + 1) * 16, cols] = both.astype(BF16)

    pl.semaphore_wait(barrier, 20)

    def s1_copy(half, g, slot):
        return pltpu.make_async_remote_copy(
            src_ref=slabs.at[group(half, g)],
            dst_ref=landed.at[half, slot],
            send_sem=s1_send.at[half, g],
            recv_sem=s1_recv.at[half, slot],
            device_id=(ring_dev(half, g), c),
            device_id_type=MESH,
        )

    def id_copy(half, g, slot):
        return pltpu.make_async_remote_copy(
            src_ref=ids.at[half, positions[half]],
            dst_ref=ids.at[half, slot],
            send_sem=id_send.at[half, g],
            recv_sem=id_recv.at[half, slot],
            device_id=(ring_dev(half, g), c),
            device_id_type=MESH,
        )

    def id_start(o):
        for half in range(2):
            g = lax.rem(positions[half] + o, RING)
            id_copy(half, g, positions[half]).start()

    def s1_out(other, offsets):
        for o in offsets:
            for half in range(2):
                g = lax.rem(lines[1 - half] + o, 4) * NCORE + other
                s1_copy(half, g, positions[half]).start()

    def s1_beside(other):
        for half in range(2):
            s1_copy(half, lines[1 - half] * NCORE + other, positions[half]).start()

    steps(1, RING, id_start)
    s1_out(0, (2, 1, 3))
    pl.when(core == 1)(lambda: s1_beside(0))
    s1_out(1, (1, 3))

    @pl.when(core == 1)
    def _():
        s1_out(1, (2,))

    @pl.when(core == 0)
    def _():
        s1_beside(1)

    def z_copy(turn, src, dst, peer, slot):
        return pltpu.make_async_remote_copy(
            src_ref=src,
            dst_ref=dst.at[slot],
            send_sem=z_send.at[turn, peer],
            recv_sem=z_recv.at[turn, slot],
            device_id=(me, peer),
            device_id_type=MESH,
        )

    def x_copy(peer, slot):
        return z_copy(0, normed_ref, x_all, peer, slot)

    loads[13].wait()
    for o in FAR_FIRST:
        x_copy(lax.rem(c + o, NZ), c).start()
    x_all[c] = normed_ref[...]
    for half in range(2):
        landed[half, positions[half]] = slabs[group(half, positions[half])]

    loads[8].wait()
    loads[9].wait()

    def fuse(i):
        mine = rows_of(i * 128, 128)
        for n in range(4):
            cols = slice(n * 256, (n + 1) * 256)
            fused[mine, cols] = jnp.dot(
                project[mine, :], adapter[:, cols], preferred_element_type=F32
            ).astype(BF16)

    steps(0, 8, fuse)

    loads[10].wait()
    for n in range(14, 18):
        loads[n].wait()
    prow = lax.broadcasted_iota(jnp.int32, (256, 256), 0)
    pcol = lax.broadcasted_iota(jnp.int32, (256, 256), 1)
    want = jnp.where(prow < 128, 2 * prow, 2 * prow - 255)
    apart = (pcol == want).astype(F32).astype(BF16)
    for b in range(8):
        both = jnp.dot(apart, expand2[b * 256 : (b + 1) * 256, :], preferred_element_type=F32)
        both = both.astype(BF16)
        expand[b * 128 : (b + 1) * 128, 0:128] = both[:128]
        expand[b * 128 : (b + 1) * 128, 128:256] = both[128:]

    lane = lax.broadcasted_iota(jnp.int32, (8, 256), 1)
    same = lax.broadcasted_iota(jnp.int32, (8, 256), 0) == lax.rem(lane, 8)
    unit = lax.div(lane, 8)
    outer = lax.div(unit, 8)
    inner = lax.rem(unit, 4)
    odd = lax.rem(lax.div(unit, 4), NCORE)
    utts = ((outer * NX + inner) * NCORE + odd, (inner * NX + outer) * NCORE + odd)
    for half in range(2):

        def id_wait(o, half=half):
            slot = lax.rem(positions[half] + o, RING)
            id_copy(half, slot, slot).wait_recv()

        steps(1, RING, id_wait)

        def choose(s, half=half):
            for r in range(8):
                row = ids[half, s, r : r + 1, :]
                wide = jnp.concatenate([row, row], axis=1)
                hit = jnp.logical_and(same, wide == utts[half])
                sel_t[rows_of(s * 64 + r * 8, 8), :] = hit.astype(F32)

        steps(0, 8, choose)
        sel[half] = sel_t[...].T.astype(BF16)

    def s2_copy(half, to, q, slot):
        return pltpu.make_async_remote_copy(
            src_ref=part.at[half, q, to],
            dst_ref=part_in.at[half, to, slot],
            send_sem=s2_send.at[half, to, q],
            recv_sem=s2_recv.at[half, to, slot],
            device_id=(line_dev(half, q), c),
            device_id_type=MESH,
        )

    for half in range(2):

        def s1_wait(o, half=half):
            slot = lax.rem(positions[half] + o, RING)
            s1_copy(half, slot, slot).wait_recv()

        steps(1, RING, s1_wait)
        for n in range(4):
            cols = slice(n * 256, (n + 1) * 256)
            got = jnp.dot(
                sel[half],
                landed[half, :, :, cols].reshape(512, 256),
                preferred_element_type=F32,
            )
            part[half, :, :, :, cols] = got.astype(BF16).reshape(4, 2, 32, 256)

        def s2_start(o, half=half):
            s2_copy(half, 0, lax.rem(lines[half] + o, 4), lines[half]).start()

        steps(1, 4, s2_start)
        for to in range(2):
            part_in[half, to, lines[half]] = part[half, lines[half], to]

    def s2_start(o):
        for half in range(2):
            s2_copy(half, 1, lax.rem(lines[half] + o, 4), lines[half]).start()

    steps(1, 4, s2_start)

    @pl.when(core == 0)
    def _():
        s1_out(1, (2,))


    steps(1, NZ, lambda o: x_copy(lax.rem(c + o, NZ), lax.rem(c + o, NZ)).wait_recv())
    both = jnp.zeros((128, 256), F32)
    for b in range(8):
        both += jnp.dot(
            x_all[b], expand[b * 128 : (b + 1) * 128, :], preferred_element_type=F32
        )
    value = both[:, :128]
    sig_gate = jax.nn.sigmoid(both[:, 128:])
    frame = lax.broadcasted_iota(jnp.int32, (128, 128), 0)
    mask = (frame < frames_sm[0]).astype(F32)
    pad[...] = jnp.zeros_like(pad)
    pad[8:136, :] = mask * value * sig_gate
    taps = taps_ref[...].astype(F32)
    depth = jnp.zeros((128, 128), F32)
    for k in range(9):
        depth += taps[k : k + 1, :] * pad[4 + k : 132 + k, :]
    shifted = depth * scale_ref[...] + shift_ref[...]
    sig_shift = jax.nn.sigmoid(shifted)
    f_gsw[...] = sig_shift * (1.0 + shifted * (1.0 - sig_shift)) * scale_ref[...] * mask
    f_val[...] = sig_gate * mask
    f_gate[...] = value * sig_gate * (1.0 - sig_gate) * mask

    def z_part(to, peer, slot):
        return z_copy(1 + to, zsend.at[to, peer], zrecv.at[to], peer, slot)

    def z_stream(peer, slot):
        return z_copy(3, wsend.at[peer], wrecv, peer, slot)

    for to in range(2):
        for half in range(2):

            def s2_wait(o, half=half, to=to):
                slot = lax.rem(lines[half] + o, 4)
                s2_copy(half, to, slot, slot).wait_recv()

            steps(1, 4, s2_wait)
            total = part_in[half, to, 0].astype(F32)
            for q in range(1, 4):
                total += part_in[half, to, q].astype(F32)
            fg[to * 64 + half * 32 : to * 64 + half * 32 + 32, :] = total.astype(BF16)

        def send_pair(n, to=to):
            got = nt(fg[to * 64 : to * 64 + 64, :], fused[rows_of(n * 256, 256), :])
            got = got.astype(BF16)
            for side in range(2):
                peer = 2 * n + side
                zsend[to, peer] = got[:, side * 128 : side * 128 + 128]

                @pl.when(peer != c)
                def _():
                    z_part(to, peer, c).start()

        for o in (2, 1, 3, 0):
            send_pair(lax.rem(lax.div(c, 2) + o, 4))
        zrecv[to, c] = zsend[to, c]

    def z_sum(copy, into):
        def hold(o):
            slot = lax.rem(c + o, NZ)
            copy(slot, slot).wait_recv()

        steps(1, NZ, hold)
        total = into[0].astype(F32)
        for b in range(1, NZ):
            total += into[b].astype(F32)
        return total

    def back_copy(kind, half, to, q, slot):
        if half == 0:
            device = y * RING + q * NCORE + to
        else:
            device = q * RING + x * NCORE + to
        return pltpu.make_async_remote_copy(
            src_ref=owned.at[kind, rows_of(to * 64 + half * 32 + q * 8, 8), :],
            dst_ref=back.at[kind, rows_of(group(half, slot) * 8, 8), :],
            send_sem=b_send.at[kind, half, to * 4 + q],
            recv_sem=b_recv.at[kind, half, slot],
            device_id=(device, c),
            device_id_type=MESH,
        )

    def give_back(kind, to):
        def go(o):
            for half in range(2):
                q = lax.rem(lines[1 - half] + o, 4)
                back_copy(kind, half, to, q, positions[half]).start()

        steps(1, 4, go)

        @pl.when(core != to)
        def _():
            for half in range(2):
                back_copy(kind, half, to, lines[1 - half], positions[half]).start()

        @pl.when(core == to)
        def _():
            for half in range(2):
                mine = rows_of(to * 64 + half * 32 + lines[1 - half] * 8, 8)
                home = rows_of(group(half, positions[half]) * 8, 8)
                back[kind, home, :] = owned[kind, mine, :]

    def back_wait(kind, other):
        def hold(o):
            for half in range(2):
                slot = lax.rem(lines[1 - half] + o, 4) * NCORE + other
                back_copy(kind, half, 0, 0, slot).wait_recv()

        steps(1, 4, hold)

        @pl.when(core != other)
        def _():
            for half in range(2):
                back_copy(kind, half, 0, 0, lines[1 - half] * NCORE + other).wait_recv()

    def last_copy(turn, peer, slot):
        rows = slice(0, 48) if turn == 0 else slice(48, 128)
        return pltpu.make_async_remote_copy(
            src_ref=fsend.at[peer, rows, :],
            dst_ref=frecv.at[slot, rows, :],
            send_sem=z_send.at[4 + turn, peer],
            recv_sem=z_recv.at[4 + turn, slot],
            device_id=(me, peer),
            device_id_type=MESH,
        )

    def last_part(turn):
        lo, hi = (0, 48) if turn == 0 else (48, 128)
        new = slice(turn * 64, turn * 64 + 64)
        pad[8 + turn * 64 : 72 + turn * 64, :] = back[0, new, :] * f_gsw[new, :]
        grad_glu = jnp.zeros((hi - lo, 128), F32)
        for k in range(9):
            grad_glu += taps[k : k + 1, :] * pad[12 - k + lo : 12 - k + hi, :]
        grad_expanded = jnp.concatenate(
            [grad_glu * f_val[lo:hi, :], grad_glu * f_gate[lo:hi, :]], axis=1
        ).astype(BF16)
        for o in (2, 1, 3, 0):
            n = lax.rem(lax.div(c, 2) + o, 4)
            got = nt(grad_expanded, expand[rows_of(n * 256, 256), :]).astype(BF16)
            for side in range(2):
                peer = 2 * n + side
                fsend[peer, lo:hi, :] = got[:, side * 128 : side * 128 + 128]

                @pl.when(peer != c)
                def _():
                    last_copy(turn, peer, c).start()

    def early():
        back_wait(0, 0)
        last_part(0)

    pl.when(core == 1)(early)

    for n in range(4):
        got = nt(fg[...], adapter[n * 256 : (n + 1) * 256, :]).astype(BF16)
        wsend[2 * n] = got[:, :128]
        wsend[2 * n + 1] = got[:, 128:]
    for o in FAR_FIRST:
        z_stream(lax.rem(c + o, NZ), c).start()
    wrecv[c] = wsend[c]

    for to in range(2):
        owned[0, to * 64 : to * 64 + 64, :] = z_sum(
            lambda peer, slot, to=to: z_part(to, peer, slot), zrecv.at[to]
        )
        give_back(0, to)
    pl.when(core == 0)(early)
    back_wait(0, 1)
    last_part(1)
    frecv[c] = fsend[c]

    owned[1] = z_sum(z_stream, wrecv)
    for to in range(2):
        give_back(1, to)
    for other in range(2):
        back_wait(1, other)
    stream_out[...] = back[1] * mask

    def last_wait(o):
        slot = lax.rem(c + o, NZ)
        for turn in range(2):
            last_copy(turn, slot, slot).wait_recv()

    steps(1, NZ, last_wait)
    total = frecv[0].astype(F32)
    for b in range(1, NZ):
        total += frecv[b].astype(F32)
    normed_out[...] = total

    def sent(o):
        peer = lax.rem(c + o, NZ)
        x_copy(peer, c).wait_send()
        z_stream(peer, c).wait_send()
        for turn in range(2):
            z_part(turn, peer, c).wait_send()
            last_copy(turn, peer, c).wait_send()
        for half in range(2):
            g = lax.rem(positions[half] + o, RING)
            s1_copy(half, g, positions[half]).wait_send()
            id_copy(half, g, positions[half]).wait_send()

    steps(1, NZ, sent)

    def sent_line(o):
        for half in range(2):
            for to in range(2):
                s2_copy(half, to, lax.rem(lines[half] + o, 4), lines[half]).wait_send()
                q = lax.rem(lines[1 - half] + o, 4)
                for kind in range(2):
                    back_copy(kind, half, to, q, positions[half]).wait_send()

    steps(1, 4, sent_line)
    for to in range(2):

        @pl.when(core != to)
        def _():
            for half in range(2):
                for kind in range(2):
                    back_copy(kind, half, to, lines[1 - half], positions[half]).wait_send()


def body(
    frame_cotangent,
    rollout_utterance,
    frame_offset,
    utterance_frames,
    normed_input,
    expand_weight,
    depth_kernel,
    norm_scale,
    norm_shift,
    project_weight,
    adapter_weight,
):
    vmem = pl.BlockSpec(memory_space=pltpu.VMEM)
    hbm = pl.BlockSpec(memory_space=pl.ANY)
    dma = pltpu.SemaphoreType.DMA
    block = jax.ShapeDtypeStruct((128, 128), F32)
    stream, normed = pl.pallas_call(
        kernel,
        out_shape=(block, block),
        in_specs=[hbm] * 11,
        out_specs=(vmem, vmem),
        scratch_shapes=[
            pltpu.SMEM((8,), jnp.int32),
            pltpu.SMEM((8,), jnp.int32),
            pltpu.SMEM((1,), jnp.int32),
            pltpu.VMEM((128, 128), BF16),
            pltpu.VMEM((9, 128), BF16),
            pltpu.VMEM((1, 128), F32),
            pltpu.VMEM((1, 128), F32),
            pltpu.VMEM((8, 160, 1024), BF16),
            pltpu.VMEM((2048, 128), BF16),
            pltpu.VMEM((1024, 1024), BF16),
            pltpu.VMEM((1024, 1024), BF16),
            pltpu.VMEM((1024, 1024), BF16),
            pltpu.VMEM((1024, 256), BF16),
            pltpu.VMEM((16, 64, 1024), BF16),
            pltpu.VMEM((2, 8, 64, 1024), BF16),
            pltpu.VMEM((2, 8, 8, 128), jnp.int32),
            pltpu.VMEM((512, 256), F32),
            pltpu.VMEM((2, 256, 512), BF16),
            pltpu.VMEM((2, 4, 2, 32, 1024), BF16),
            pltpu.VMEM((2, 2, 4, 32, 1024), BF16),
            pltpu.VMEM((128, 1024), BF16),
            pltpu.VMEM((8, 128, 128), BF16),
            pltpu.VMEM((2, 8, 64, 128), BF16),
            pltpu.VMEM((2, 8, 64, 128), BF16),
            pltpu.VMEM((8, 128, 128), BF16),
            pltpu.VMEM((8, 128, 128), BF16),
            pltpu.VMEM((8, 128, 128), BF16),
            pltpu.VMEM((8, 128, 128), BF16),
            pltpu.VMEM((2, 128, 128), F32),
            pltpu.VMEM((2, 128, 128), F32),
            pltpu.VMEM((144, 128), F32),
            pltpu.VMEM((128, 128), F32),
            pltpu.VMEM((128, 128), F32),
            pltpu.VMEM((128, 128), F32),
            dma((18,)),
            dma((2, 8)),
            dma((2, 8)),
            dma((2, 8)),
            dma((2, 8)),
            dma((2, 2, 4)),
            dma((2, 2, 4)),
            dma((6, 8)),
            dma((6, 8)),
            dma((2, 2, 8)),
            dma((2, 2, 8)),
        ],
        compiler_params=pltpu.CompilerParams(
            collective_id=0, has_side_effects=True, vmem_limit_bytes=63 * 1024 * 1024
        ),
        cost_estimate=pl.CostEstimate(
            flops=5_000_000_000, bytes_accessed=8_000_000, transcendentals=40_000
        ),
    )(
        rollout_utterance,
        frame_offset,
        utterance_frames,
        normed_input.reshape(128, 128),
        depth_kernel,
        norm_scale.reshape(1, 128),
        norm_shift.reshape(1, 128),
        frame_cotangent,
        expand_weight.reshape(2048, 128),
        project_weight,
        adapter_weight,
    )
    stream, normed = lax.optimization_barrier((stream, normed))
    return stream.reshape(1, 128, 128).astype(BF16), normed.reshape(1, 128, 128).astype(BF16)


def solution(mesh):
    return jax.shard_map(
        body,
        mesh=mesh,
        in_specs=(
            P("dec", None, "ch"),
            P("dec"),
            P("dec"),
            P("dec"),
            P("dec", None, "ch"),
            P(None, None, "ch"),
            P(None, "ch"),
            P("ch"),
            P("ch"),
            P(),
            P(None, "ch"),
        ),
        out_specs=(P("dec", None, "ch"), P("dec", None, "ch")),
        check_vma=False,
    )
```

```python
import jax
import jax.numpy as jnp
from jax import lax
from jax.experimental import pallas as pl
from jax.experimental.pallas import tpu as pltpu
from jax.sharding import PartitionSpec as P

MESH = pl.DeviceIdType.MESH
F32 = jnp.float32
BF16 = jnp.bfloat16
NY, NX, NCORE, NZ = 4, 4, 2, 8
FAR_FIRST = (4, 3, 5, 2, 6, 1, 7)
RING = NX * NCORE


def steps(first, last, work):
    def one(step, carry):
        work(step)
        return carry

    lax.fori_loop(first, last, one, 0)


def rows_of(start, size):
    return pl.ds(pl.multiple_of(start, size), size)


def nt(a, b):
    return lax.dot_general(a, b, (((1,), (1,)), ((), ())), preferred_element_type=F32)


def kernel(
    ids_hbm,
    offs_hbm,
    frames_hbm,
    normed_hbm,
    taps_hbm,
    scale_hbm,
    shift_hbm,
    cot_hbm,
    expand_hbm,
    project_hbm,
    adapter_hbm,
    stream_out,
    normed_out,
    ids_sm,
    offs_sm,
    frames_sm,
    normed_ref,
    taps_ref,
    scale_ref,
    shift_ref,
    cot,
    expand2,
    project,
    adapter,
    fused,
    expand,
    slabs,
    landed,
    ids,
    sel_t,
    sel,
    part,
    part_in,
    fg,
    x_all,
    zsend,
    zrecv,
    wsend,
    wrecv,
    fsend,
    frecv,
    owned,
    back,
    pad,
    f_gsw,
    f_val,
    f_gate,
    load_sem,
    s1_send,
    s1_recv,
    id_send,
    id_recv,
    s2_send,
    s2_recv,
    z_send,
    z_recv,
    b_send,
    b_recv,
):
    me = lax.axis_index("dec")
    c = lax.axis_index("ch")
    y = lax.div(me, RING)
    pos_a = lax.rem(me, RING)
    x = lax.div(pos_a, NCORE)
    core = lax.rem(pos_a, NCORE)
    pos_b = y * NCORE + core
    positions = (pos_a, pos_b)

    def group(half, g):
        return lax.rem(g, NCORE) * 8 + half * 4 + lax.div(g, NCORE)

    def ring_dev(half, g):
        if half == 0:
            return y * RING + g
        return lax.div(g, NCORE) * RING + x * NCORE + lax.rem(g, NCORE)

    def line_dev(half, q):
        if half == 0:
            return q * RING + pos_a
        return y * RING + q * NCORE + core

    lines = (y, x)

    small = (
        (offs_hbm, offs_sm),
        (ids_hbm, ids_sm),
        (normed_hbm, normed_ref),
        (frames_hbm, frames_sm),
        (taps_hbm, taps_ref),
        (scale_hbm, scale_ref),
        (shift_hbm, shift_ref),
    )
    pairs = [(cot_hbm.at[2 * p : 2 * p + 2], cot.at[2 * p : 2 * p + 2]) for p in range(4)]
    pairs += [(project_hbm, project), (adapter_hbm, adapter), (expand_hbm, expand2)]
    pairs += small
    loads = [pltpu.make_async_copy(a, b, load_sem.at[n]) for n, (a, b) in enumerate(pairs)]
    for n in (7, 8, 0, 1, 2, 3):
        loads[n].start()

    barrier = pltpu.get_barrier_semaphore()

    def greet(device):
        pl.semaphore_signal(barrier, inc=1, device_id=device, device_id_type=MESH)

    steps(1, RING, lambda o: greet((ring_dev(0, lax.rem(pos_a + o, RING)), c)))
    for other in range(NCORE):
        steps(1, NY, lambda o: greet((ring_dev(1, lax.rem(y + o, NY) * NCORE + other), c)))
    steps(1, NZ, lambda o: greet((me, lax.rem(c + o, NZ))))

    for n in (9, 4, 5, 6, 10, 11, 12, 13):
        loads[n].start()
    loads[7].wait()
    loads[8].wait()
    row8 = lax.broadcasted_iota(jnp.int32, (8, 128), 0)
    tile = jnp.zeros((8, 128), jnp.int32)
    for r in range(8):
        tile = jnp.where(row8 == r, ids_sm[r], tile)
    ids[0, pos_a] = tile
    ids[1, pos_b] = tile

    srow = lax.broadcasted_iota(jnp.int32, (128, 160), 0)
    scol = lax.broadcasted_iota(jnp.int32, (128, 160), 1)
    diff = scol - srow
    for p in range(4):
        loads[p].wait()
        sh0 = (diff == offs_sm[2 * p]).astype(F32).astype(BF16)
        sh1 = (diff == offs_sm[2 * p + 1]).astype(F32).astype(BF16)
        for n in range(4):
            cols = slice(n * 256, (n + 1) * 256)
            a = jnp.dot(sh0, cot[2 * p, :, cols], preferred_element_type=F32)
            b = jnp.dot(sh1, cot[2 * p + 1, :, cols], preferred_element_type=F32)
            both = jnp.concatenate([a.reshape(16, 8, 256), b.reshape(16, 8, 256)], axis=1)
            slabs[:, p * 16 : (p + 1) * 16, cols] = both.astype(BF16)

    pl.semaphore_wait(barrier, 20)

    def s1_copy(half, g, slot):
        return pltpu.make_async_remote_copy(
            src_ref=slabs.at[group(half, g)],
            dst_ref=landed.at[half, slot],
            send_sem=s1_send.at[half, g],
            recv_sem=s1_recv.at[half, slot],
            device_id=(ring_dev(half, g), c),
            device_id_type=MESH,
        )

    def id_copy(half, g, slot):
        return pltpu.make_async_remote_copy(
            src_ref=ids.at[half, positions[half]],
            dst_ref=ids.at[half, slot],
            send_sem=id_send.at[half, g],
            recv_sem=id_recv.at[half, slot],
            device_id=(ring_dev(half, g), c),
            device_id_type=MESH,
        )

    def id_start(o):
        for half in range(2):
            g = lax.rem(positions[half] + o, RING)
            id_copy(half, g, positions[half]).start()

    def s1_out(other, offsets):
        for o in offsets:
            for half in range(2):
                g = lax.rem(lines[1 - half] + o, 4) * NCORE + other
                s1_copy(half, g, positions[half]).start()

    def s1_beside(other):
        for half in range(2):
            s1_copy(half, lines[1 - half] * NCORE + other, positions[half]).start()

    s1_out(0, (2,))
    steps(1, RING, id_start)
    s1_out(0, (1, 3))
    pl.when(core == 1)(lambda: s1_beside(0))
    s1_out(1, (1, 3))

    @pl.when(core == 1)
    def _():
        s1_out(1, (2,))

    @pl.when(core == 0)
    def _():
        s1_beside(1)

    def z_copy(turn, src, dst, peer, slot):
        return pltpu.make_async_remote_copy(
            src_ref=src,
            dst_ref=dst.at[slot],
            send_sem=z_send.at[turn, peer],
            recv_sem=z_recv.at[turn, slot],
            device_id=(me, peer),
            device_id_type=MESH,
        )

    def x_copy(peer, slot):
        return z_copy(0, normed_ref, x_all, peer, slot)

    loads[9].wait()
    for o in FAR_FIRST:
        x_copy(lax.rem(c + o, NZ), c).start()
    x_all[c] = normed_ref[...]
    for half in range(2):
        landed[half, positions[half]] = slabs[group(half, positions[half])]

    loads[4].wait()
    loads[5].wait()

    def fuse(i):
        mine = rows_of(i * 128, 128)
        for n in range(4):
            cols = slice(n * 256, (n + 1) * 256)
            fused[mine, cols] = jnp.dot(
                project[mine, :], adapter[:, cols], preferred_element_type=F32
            ).astype(BF16)

    steps(0, 8, fuse)

    loads[6].wait()
    for n in range(10, 14):
        loads[n].wait()
    prow = lax.broadcasted_iota(jnp.int32, (256, 256), 0)
    pcol = lax.broadcasted_iota(jnp.int32, (256, 256), 1)
    want = jnp.where(prow < 128, 2 * prow, 2 * prow - 255)
    apart = (pcol == want).astype(F32).astype(BF16)
    for b in range(8):
        both = jnp.dot(apart, expand2[b * 256 : (b + 1) * 256, :], preferred_element_type=F32)
        both = both.astype(BF16)
        expand[b * 128 : (b + 1) * 128, 0:128] = both[:128]
        expand[b * 128 : (b + 1) * 128, 128:256] = both[128:]

    lane = lax.broadcasted_iota(jnp.int32, (8, 256), 1)
    same = lax.broadcasted_iota(jnp.int32, (8, 256), 0) == lax.rem(lane, 8)
    unit = lax.div(lane, 8)
    outer = lax.div(unit, 8)
    inner = lax.rem(unit, 4)
    odd = lax.rem(lax.div(unit, 4), NCORE)
    utts = ((outer * NX + inner) * NCORE + odd, (inner * NX + outer) * NCORE + odd)
    for half in range(2):

        def id_wait(o, half=half):
            slot = lax.rem(positions[half] + o, RING)
            id_copy(half, slot, slot).wait_recv()

        steps(1, RING, id_wait)

        def choose(s, half=half):
            for r in range(8):
                row = ids[half, s, r : r + 1, :]
                wide = jnp.concatenate([row, row], axis=1)
                hit = jnp.logical_and(same, wide == utts[half])
                sel_t[rows_of(s * 64 + r * 8, 8), :] = hit.astype(F32)

        steps(0, 8, choose)
        sel[half] = sel_t[...].T.astype(BF16)

    def s2_copy(half, to, q, slot):
        return pltpu.make_async_remote_copy(
            src_ref=part.at[half, q, to],
            dst_ref=part_in.at[half, to, slot],
            send_sem=s2_send.at[half, to, q],
            recv_sem=s2_recv.at[half, to, slot],
            device_id=(line_dev(half, q), c),
            device_id_type=MESH,
        )

    for half in range(2):

        def s1_wait(o, half=half):
            slot = lax.rem(positions[half] + o, RING)
            s1_copy(half, slot, slot).wait_recv()

        steps(1, RING, s1_wait)
        for n in range(4):
            cols = slice(n * 256, (n + 1) * 256)
            got = jnp.dot(
                sel[half],
                landed[half, :, :, cols].reshape(512, 256),
                preferred_element_type=F32,
            )
            part[half, :, :, :, cols] = got.astype(BF16).reshape(4, 2, 32, 256)

        def s2_start(o, half=half):
            s2_copy(half, 0, lax.rem(lines[half] + o, 4), lines[half]).start()

        for o in (2, 1, 3):
            s2_start(o)
        for to in range(2):
            part_in[half, to, lines[half]] = part[half, lines[half], to]

    def s2_start(o):
        for half in range(2):
            s2_copy(half, 1, lax.rem(lines[half] + o, 4), lines[half]).start()

    for o in (2, 1, 3):
        s2_start(o)

    @pl.when(core == 0)
    def _():
        s1_out(1, (2,))


    steps(1, NZ, lambda o: x_copy(lax.rem(c + o, NZ), lax.rem(c + o, NZ)).wait_recv())
    both = jnp.zeros((128, 256), F32)
    for b in range(8):
        both += jnp.dot(
            x_all[b], expand[b * 128 : (b + 1) * 128, :], preferred_element_type=F32
        )
    value = both[:, :128]
    sig_gate = jax.nn.sigmoid(both[:, 128:])
    frame = lax.broadcasted_iota(jnp.int32, (128, 128), 0)
    mask = (frame < frames_sm[0]).astype(F32)
    pad[...] = jnp.zeros_like(pad)
    pad[8:136, :] = mask * value * sig_gate
    taps = taps_ref[...].astype(F32)
    depth = jnp.zeros((128, 128), F32)
    for k in range(9):
        depth += taps[k : k + 1, :] * pad[4 + k : 132 + k, :]
    shifted = depth * scale_ref[...] + shift_ref[...]
    sig_shift = jax.nn.sigmoid(shifted)
    f_gsw[...] = sig_shift * (1.0 + shifted * (1.0 - sig_shift)) * scale_ref[...] * mask
    f_val[...] = sig_gate * mask
    f_gate[...] = value * sig_gate * (1.0 - sig_gate) * mask

    def z_part(to, peer, slot):
        return z_copy(1 + to, zsend.at[to, peer], zrecv.at[to], peer, slot)

    def z_stream(peer, slot):
        return z_copy(3, wsend.at[peer], wrecv, peer, slot)

    for to in range(2):
        for half in range(2):

            def s2_wait(o, half=half, to=to):
                slot = lax.rem(lines[half] + o, 4)
                s2_copy(half, to, slot, slot).wait_recv()

            steps(1, 4, s2_wait)
            total = part_in[half, to, 0].astype(F32)
            for q in range(1, 4):
                total += part_in[half, to, q].astype(F32)
            fg[to * 64 + half * 32 : to * 64 + half * 32 + 32, :] = total.astype(BF16)

        def send_pair(n, to=to):
            got = nt(fg[to * 64 : to * 64 + 64, :], fused[rows_of(n * 256, 256), :])
            got = got.astype(BF16)
            for side in range(2):
                peer = 2 * n + side
                zsend[to, peer] = got[:, side * 128 : side * 128 + 128]

                @pl.when(peer != c)
                def _():
                    z_part(to, peer, c).start()

        for o in (2, 1, 3, 0):
            send_pair(lax.rem(lax.div(c, 2) + o, 4))
        zrecv[to, c] = zsend[to, c]

    def z_sum(copy, into):
        def hold(o):
            slot = lax.rem(c + o, NZ)
            copy(slot, slot).wait_recv()

        steps(1, NZ, hold)
        total = into[0].astype(F32)
        for b in range(1, NZ):
            total += into[b].astype(F32)
        return total

    def back_copy(kind, half, to, q, slot):
        if half == 0:
            device = y * RING + q * NCORE + to
        else:
            device = q * RING + x * NCORE + to
        return pltpu.make_async_remote_copy(
            src_ref=owned.at[kind, rows_of(to * 64 + half * 32 + q * 8, 8), :],
            dst_ref=back.at[kind, rows_of(group(half, slot) * 8, 8), :],
            send_sem=b_send.at[kind, half, to * 4 + q],
            recv_sem=b_recv.at[kind, half, slot],
            device_id=(device, c),
            device_id_type=MESH,
        )

    def give_back(kind, to):
        def go(o):
            for half in range(2):
                q = lax.rem(lines[1 - half] + o, 4)
                back_copy(kind, half, to, q, positions[half]).start()

        for o in (2, 1, 3):
            go(o)

        @pl.when(core != to)
        def _():
            for half in range(2):
                back_copy(kind, half, to, lines[1 - half], positions[half]).start()

        @pl.when(core == to)
        def _():
            for half in range(2):
                mine = rows_of(to * 64 + half * 32 + lines[1 - half] * 8, 8)
                home = rows_of(group(half, positions[half]) * 8, 8)
                back[kind, home, :] = owned[kind, mine, :]

    def back_wait(kind, other):
        def hold(o):
            for half in range(2):
                slot = lax.rem(lines[1 - half] + o, 4) * NCORE + other
                back_copy(kind, half, 0, 0, slot).wait_recv()

        steps(1, 4, hold)

        @pl.when(core != other)
        def _():
            for half in range(2):
                back_copy(kind, half, 0, 0, lines[1 - half] * NCORE + other).wait_recv()

    def last_copy(turn, peer, slot):
        rows = slice(0, 48) if turn == 0 else slice(48, 128)
        return pltpu.make_async_remote_copy(
            src_ref=fsend.at[peer, rows, :],
            dst_ref=frecv.at[slot, rows, :],
            send_sem=z_send.at[4 + turn, peer],
            recv_sem=z_recv.at[4 + turn, slot],
            device_id=(me, peer),
            device_id_type=MESH,
        )

    def last_part(turn):
        lo, hi = (0, 48) if turn == 0 else (48, 128)
        new = slice(turn * 64, turn * 64 + 64)
        pad[8 + turn * 64 : 72 + turn * 64, :] = back[0, new, :] * f_gsw[new, :]
        grad_glu = jnp.zeros((hi - lo, 128), F32)
        for k in range(9):
            grad_glu += taps[k : k + 1, :] * pad[12 - k + lo : 12 - k + hi, :]
        grad_expanded = jnp.concatenate(
            [grad_glu * f_val[lo:hi, :], grad_glu * f_gate[lo:hi, :]], axis=1
        ).astype(BF16)
        for o in (2, 1, 3, 0):
            n = lax.rem(lax.div(c, 2) + o, 4)
            got = nt(grad_expanded, expand[rows_of(n * 256, 256), :]).astype(BF16)
            for side in range(2):
                peer = 2 * n + side
                fsend[peer, lo:hi, :] = got[:, side * 128 : side * 128 + 128]

                @pl.when(peer != c)
                def _():
                    last_copy(turn, peer, c).start()

    def early():
        back_wait(0, 0)
        last_part(0)

    pl.when(core == 1)(early)

    for n in range(4):
        got = nt(fg[...], adapter[n * 256 : (n + 1) * 256, :]).astype(BF16)
        wsend[2 * n] = got[:, :128]
        wsend[2 * n + 1] = got[:, 128:]
    for o in FAR_FIRST:
        z_stream(lax.rem(c + o, NZ), c).start()
    wrecv[c] = wsend[c]

    for to in range(2):
        owned[0, to * 64 : to * 64 + 64, :] = z_sum(
            lambda peer, slot, to=to: z_part(to, peer, slot), zrecv.at[to]
        )
        give_back(0, to)
    pl.when(core == 0)(early)
    back_wait(0, 1)
    last_part(1)
    frecv[c] = fsend[c]

    owned[1] = z_sum(z_stream, wrecv)
    for to in range(2):
        give_back(1, to)
    for other in range(2):
        back_wait(1, other)
    stream_out[...] = back[1] * mask

    for turn in range(2):
        lo, hi = (0, 48) if turn == 0 else (48, 128)

        def last_wait(o, turn=turn):
            slot = lax.rem(c + o, NZ)
            last_copy(turn, slot, slot).wait_recv()

        steps(1, NZ, last_wait)
        total = frecv[0, lo:hi, :].astype(F32)
        for b in range(1, NZ):
            total += frecv[b, lo:hi, :].astype(F32)
        normed_out[lo:hi, :] = total

    def sent(o):
        peer = lax.rem(c + o, NZ)
        x_copy(peer, c).wait_send()
        z_stream(peer, c).wait_send()
        for turn in range(2):
            z_part(turn, peer, c).wait_send()
            last_copy(turn, peer, c).wait_send()
        for half in range(2):
            g = lax.rem(positions[half] + o, RING)
            s1_copy(half, g, positions[half]).wait_send()
            id_copy(half, g, positions[half]).wait_send()

    steps(1, NZ, sent)

    def sent_line(o):
        for half in range(2):
            for to in range(2):
                s2_copy(half, to, lax.rem(lines[half] + o, 4), lines[half]).wait_send()
                q = lax.rem(lines[1 - half] + o, 4)
                for kind in range(2):
                    back_copy(kind, half, to, q, positions[half]).wait_send()

    steps(1, 4, sent_line)
    for to in range(2):

        @pl.when(core != to)
        def _():
            for half in range(2):
                for kind in range(2):
                    back_copy(kind, half, to, lines[1 - half], positions[half]).wait_send()


def body(
    frame_cotangent,
    rollout_utterance,
    frame_offset,
    utterance_frames,
    normed_input,
    expand_weight,
    depth_kernel,
    norm_scale,
    norm_shift,
    project_weight,
    adapter_weight,
):
    vmem = pl.BlockSpec(memory_space=pltpu.VMEM)
    hbm = pl.BlockSpec(memory_space=pl.ANY)
    dma = pltpu.SemaphoreType.DMA
    block = jax.ShapeDtypeStruct((128, 128), F32)
    stream, normed = pl.pallas_call(
        kernel,
        out_shape=(block, block),
        in_specs=[hbm] * 11,
        out_specs=(vmem, vmem),
        scratch_shapes=[
            pltpu.SMEM((8,), jnp.int32),
            pltpu.SMEM((8,), jnp.int32),
            pltpu.SMEM((1,), jnp.int32),
            pltpu.VMEM((128, 128), BF16),
            pltpu.VMEM((9, 128), BF16),
            pltpu.VMEM((1, 128), F32),
            pltpu.VMEM((1, 128), F32),
            pltpu.VMEM((8, 160, 1024), BF16),
            pltpu.VMEM((2048, 128), BF16),
            pltpu.VMEM((1024, 1024), BF16),
            pltpu.VMEM((1024, 1024), BF16),
            pltpu.VMEM((1024, 1024), BF16),
            pltpu.VMEM((1024, 256), BF16),
            pltpu.VMEM((16, 64, 1024), BF16),
            pltpu.VMEM((2, 8, 64, 1024), BF16),
            pltpu.VMEM((2, 8, 8, 128), jnp.int32),
            pltpu.VMEM((512, 256), F32),
            pltpu.VMEM((2, 256, 512), BF16),
            pltpu.VMEM((2, 4, 2, 32, 1024), BF16),
            pltpu.VMEM((2, 2, 4, 32, 1024), BF16),
            pltpu.VMEM((128, 1024), BF16),
            pltpu.VMEM((8, 128, 128), BF16),
            pltpu.VMEM((2, 8, 64, 128), BF16),
            pltpu.VMEM((2, 8, 64, 128), BF16),
            pltpu.VMEM((8, 128, 128), BF16),
            pltpu.VMEM((8, 128, 128), BF16),
            pltpu.VMEM((8, 128, 128), BF16),
            pltpu.VMEM((8, 128, 128), BF16),
            pltpu.VMEM((2, 128, 128), F32),
            pltpu.VMEM((2, 128, 128), F32),
            pltpu.VMEM((144, 128), F32),
            pltpu.VMEM((128, 128), F32),
            pltpu.VMEM((128, 128), F32),
            pltpu.VMEM((128, 128), F32),
            dma((14,)),
            dma((2, 8)),
            dma((2, 8)),
            dma((2, 8)),
            dma((2, 8)),
            dma((2, 2, 4)),
            dma((2, 2, 4)),
            dma((6, 8)),
            dma((6, 8)),
            dma((2, 2, 8)),
            dma((2, 2, 8)),
        ],
        compiler_params=pltpu.CompilerParams(
            collective_id=0, has_side_effects=True, vmem_limit_bytes=63 * 1024 * 1024
        ),
        cost_estimate=pl.CostEstimate(
            flops=5_000_000_000, bytes_accessed=8_000_000, transcendentals=40_000
        ),
    )(
        rollout_utterance,
        frame_offset,
        utterance_frames,
        normed_input.reshape(128, 128),
        depth_kernel,
        norm_scale.reshape(1, 128),
        norm_shift.reshape(1, 128),
        frame_cotangent,
        expand_weight.reshape(2048, 128),
        project_weight,
        adapter_weight,
    )
    stream, normed = lax.optimization_barrier((stream, normed))
    return stream.reshape(1, 128, 128).astype(BF16), normed.reshape(1, 128, 128).astype(BF16)


def solution(mesh):
    return jax.shard_map(
        body,
        mesh=mesh,
        in_specs=(
            P("dec", None, "ch"),
            P("dec"),
            P("dec"),
            P("dec"),
            P("dec", None, "ch"),
            P(None, None, "ch"),
            P(None, "ch"),
            P("ch"),
            P("ch"),
            P(),
            P(None, "ch"),
        ),
        out_specs=(P("dec", None, "ch"), P("dec", None, "ch")),
        check_vma=False,
    )
```

```python
import jax
import jax.numpy as jnp
from jax import lax
from jax.experimental import pallas as pl
from jax.experimental.pallas import tpu as pltpu
from jax.sharding import PartitionSpec as P

MESH = pl.DeviceIdType.MESH
F32 = jnp.float32
BF16 = jnp.bfloat16
NY, NX, NCORE, NZ = 4, 4, 2, 8
FAR_FIRST = (4, 3, 5, 2, 6, 1, 7)
RING = NX * NCORE


def steps(first, last, work):
    def one(step, carry):
        work(step)
        return carry

    lax.fori_loop(first, last, one, 0)


def rows_of(start, size):
    return pl.ds(pl.multiple_of(start, size), size)


def nt(a, b):
    return lax.dot_general(a, b, (((1,), (1,)), ((), ())), preferred_element_type=F32)


def kernel(
    ids_hbm,
    offs_hbm,
    frames_hbm,
    normed_hbm,
    taps_hbm,
    scale_hbm,
    shift_hbm,
    cot_hbm,
    expand_hbm,
    project_hbm,
    adapter_hbm,
    stream_out,
    normed_out,
    ids_sm,
    offs_sm,
    frames_sm,
    normed_ref,
    taps_ref,
    scale_ref,
    shift_ref,
    cot,
    expand2,
    project,
    adapter,
    fused,
    expand,
    slabs,
    landed,
    ids,
    sel_t,
    sel,
    part,
    part_in,
    fg,
    x_all,
    zsend,
    zrecv,
    wsend,
    wrecv,
    fsend,
    frecv,
    owned,
    back,
    pad,
    f_gsw,
    f_val,
    f_gate,
    load_sem,
    s1_send,
    s1_recv,
    id_send,
    id_recv,
    s2_send,
    s2_recv,
    z_send,
    z_recv,
    b_send,
    b_recv,
):
    me = lax.axis_index("dec")
    c = lax.axis_index("ch")
    y = lax.div(me, RING)
    pos_a = lax.rem(me, RING)
    x = lax.div(pos_a, NCORE)
    core = lax.rem(pos_a, NCORE)
    pos_b = y * NCORE + core
    positions = (pos_a, pos_b)

    def group(half, g):
        return lax.rem(g, NCORE) * 8 + half * 4 + lax.div(g, NCORE)

    def ring_dev(half, g):
        if half == 0:
            return y * RING + g
        return lax.div(g, NCORE) * RING + x * NCORE + lax.rem(g, NCORE)

    def line_dev(half, q):
        if half == 0:
            return q * RING + pos_a
        return y * RING + q * NCORE + core

    lines = (y, x)

    small = (
        (offs_hbm, offs_sm),
        (ids_hbm, ids_sm),
        (normed_hbm, normed_ref),
        (frames_hbm, frames_sm),
        (taps_hbm, taps_ref),
        (scale_hbm, scale_ref),
        (shift_hbm, shift_ref),
    )
    pairs = [(cot_hbm.at[2 * p : 2 * p + 2], cot.at[2 * p : 2 * p + 2]) for p in range(4)]
    pairs += [(project_hbm, project), (adapter_hbm, adapter), (expand_hbm, expand2)]
    pairs += small
    loads = [pltpu.make_async_copy(a, b, load_sem.at[n]) for n, (a, b) in enumerate(pairs)]
    for n in (7, 8, 0, 1, 2, 3):
        loads[n].start()

    barrier = pltpu.get_barrier_semaphore()

    def greet(device):
        pl.semaphore_signal(barrier, inc=1, device_id=device, device_id_type=MESH)

    steps(1, RING, lambda o: greet((ring_dev(0, lax.rem(pos_a + o, RING)), c)))
    for other in range(NCORE):
        steps(1, NY, lambda o: greet((ring_dev(1, lax.rem(y + o, NY) * NCORE + other), c)))
    steps(1, NZ, lambda o: greet((me, lax.rem(c + o, NZ))))

    for n in (9, 4, 5, 6, 10, 11, 12, 13):
        loads[n].start()
    loads[7].wait()
    loads[8].wait()
    row8 = lax.broadcasted_iota(jnp.int32, (8, 128), 0)
    tile = jnp.zeros((8, 128), jnp.int32)
    for r in range(8):
        tile = jnp.where(row8 == r, ids_sm[r], tile)
    ids[0, pos_a] = tile
    ids[1, pos_b] = tile

    srow = lax.broadcasted_iota(jnp.int32, (128, 160), 0)
    scol = lax.broadcasted_iota(jnp.int32, (128, 160), 1)
    diff = scol - srow
    for p in range(4):
        loads[p].wait()
        sh0 = (diff == offs_sm[2 * p]).astype(F32).astype(BF16)
        sh1 = (diff == offs_sm[2 * p + 1]).astype(F32).astype(BF16)
        for n in range(4):
            cols = slice(n * 256, (n + 1) * 256)
            a = jnp.dot(sh0, cot[2 * p, :, cols], preferred_element_type=F32)
            b = jnp.dot(sh1, cot[2 * p + 1, :, cols], preferred_element_type=F32)
            both = jnp.concatenate([a.reshape(16, 8, 256), b.reshape(16, 8, 256)], axis=1)
            slabs[:, p * 16 : (p + 1) * 16, cols] = both.astype(BF16)

    pl.semaphore_wait(barrier, 20)

    def s1_copy(half, g, slot):
        return pltpu.make_async_remote_copy(
            src_ref=slabs.at[group(half, g)],
            dst_ref=landed.at[half, slot],
            send_sem=s1_send.at[half, g],
            recv_sem=s1_recv.at[half, slot],
            device_id=(ring_dev(half, g), c),
            device_id_type=MESH,
        )

    def id_copy(half, g, slot):
        return pltpu.make_async_remote_copy(
            src_ref=ids.at[half, positions[half]],
            dst_ref=ids.at[half, slot],
            send_sem=id_send.at[half, g],
            recv_sem=id_recv.at[half, slot],
            device_id=(ring_dev(half, g), c),
            device_id_type=MESH,
        )

    def id_start(o):
        for half in range(2):
            g = lax.rem(positions[half] + o, RING)
            id_copy(half, g, positions[half]).start()

    def s1_out(other, offsets):
        for o in offsets:
            for half in range(2):
                g = lax.rem(lines[1 - half] + o, 4) * NCORE + other
                s1_copy(half, g, positions[half]).start()

    def s1_beside(other):
        for half in range(2):
            s1_copy(half, lines[1 - half] * NCORE + other, positions[half]).start()

    s1_out(0, (2,))
    steps(1, RING, id_start)
    s1_out(0, (1, 3))
    pl.when(core == 1)(lambda: s1_beside(0))
    s1_out(1, (1, 3))

    @pl.when(core == 1)
    def _():
        s1_out(1, (2,))

    @pl.when(core == 0)
    def _():
        s1_beside(1)

    def z_copy(turn, src, dst, peer, slot):
        return pltpu.make_async_remote_copy(
            src_ref=src,
            dst_ref=dst.at[slot],
            send_sem=z_send.at[turn, peer],
            recv_sem=z_recv.at[turn, slot],
            device_id=(me, peer),
            device_id_type=MESH,
        )

    def x_copy(peer, slot):
        return z_copy(0, normed_ref, x_all, peer, slot)

    loads[9].wait()
    for o in FAR_FIRST:
        x_copy(lax.rem(c + o, NZ), c).start()
    x_all[c] = normed_ref[...]
    for half in range(2):
        landed[half, positions[half]] = slabs[group(half, positions[half])]

    loads[4].wait()
    loads[5].wait()

    def fuse(i):
        mine = rows_of(i * 128, 128)
        for n in range(4):
            cols = slice(n * 256, (n + 1) * 256)
            fused[mine, cols] = jnp.dot(
                project[mine, :], adapter[:, cols], preferred_element_type=F32
            ).astype(BF16)

    steps(0, 8, fuse)

    loads[6].wait()
    for n in range(10, 14):
        loads[n].wait()
    prow = lax.broadcasted_iota(jnp.int32, (256, 256), 0)
    pcol = lax.broadcasted_iota(jnp.int32, (256, 256), 1)
    want = jnp.where(prow < 128, 2 * prow, 2 * prow - 255)
    apart = (pcol == want).astype(F32).astype(BF16)
    for b in range(8):
        both = jnp.dot(apart, expand2[b * 256 : (b + 1) * 256, :], preferred_element_type=F32)
        both = both.astype(BF16)
        expand[b * 128 : (b + 1) * 128, 0:128] = both[:128]
        expand[b * 128 : (b + 1) * 128, 128:256] = both[128:]

    lane = lax.broadcasted_iota(jnp.int32, (8, 256), 1)
    same = lax.broadcasted_iota(jnp.int32, (8, 256), 0) == lax.rem(lane, 8)
    unit = lax.div(lane, 8)
    outer = lax.rem(lax.div(unit, 4), 4)
    inner = lax.rem(unit, 4)
    odd = lax.div(unit, 16)
    utts = ((outer * NX + inner) * NCORE + odd, (inner * NX + outer) * NCORE + odd)
    for half in range(2):

        def id_wait(o, half=half):
            slot = lax.rem(positions[half] + o, RING)
            id_copy(half, slot, slot).wait_recv()

        steps(1, RING, id_wait)

        def choose(s, half=half):
            for r in range(8):
                row = ids[half, s, r : r + 1, :]
                wide = jnp.concatenate([row, row], axis=1)
                hit = jnp.logical_and(same, wide == utts[half])
                sel_t[rows_of(s * 64 + r * 8, 8), :] = hit.astype(F32)

        steps(0, 8, choose)
        sel[half] = sel_t[...].T.astype(BF16)

    def s2_copy(half, to, q, slot):
        return pltpu.make_async_remote_copy(
            src_ref=part.at[half, q, to],
            dst_ref=part_in.at[half, to, slot],
            send_sem=s2_send.at[half, to, q],
            recv_sem=s2_recv.at[half, to, slot],
            device_id=(line_dev(half, q), c),
            device_id_type=MESH,
        )

    for to in range(2):
        for half in range(2):
            if to == 0:

                def s1_wait(o, half=half):
                    slot = lax.rem(positions[half] + o, RING)
                    s1_copy(half, slot, slot).wait_recv()

                steps(1, RING, s1_wait)
            for n in range(4):
                cols = slice(n * 256, (n + 1) * 256)
                got = jnp.dot(
                    sel[half, to * 128 : to * 128 + 128, :],
                    landed[half, :, :, cols].reshape(512, 256),
                    preferred_element_type=F32,
                )
                part[half, :, to, :, cols] = got.astype(BF16).reshape(4, 32, 256)
            for o in (2, 1, 3):
                s2_copy(half, to, lax.rem(lines[half] + o, 4), lines[half]).start()
            part_in[half, to, lines[half]] = part[half, lines[half], to]

    @pl.when(core == 0)
    def _():
        s1_out(1, (2,))


    steps(1, NZ, lambda o: x_copy(lax.rem(c + o, NZ), lax.rem(c + o, NZ)).wait_recv())
    both = jnp.zeros((128, 256), F32)
    for b in range(8):
        both += jnp.dot(
            x_all[b], expand[b * 128 : (b + 1) * 128, :], preferred_element_type=F32
        )
    value = both[:, :128]
    sig_gate = jax.nn.sigmoid(both[:, 128:])
    frame = lax.broadcasted_iota(jnp.int32, (128, 128), 0)
    mask = (frame < frames_sm[0]).astype(F32)
    pad[...] = jnp.zeros_like(pad)
    pad[8:136, :] = mask * value * sig_gate
    taps = taps_ref[...].astype(F32)
    depth = jnp.zeros((128, 128), F32)
    for k in range(9):
        depth += taps[k : k + 1, :] * pad[4 + k : 132 + k, :]
    shifted = depth * scale_ref[...] + shift_ref[...]
    sig_shift = jax.nn.sigmoid(shifted)
    f_gsw[...] = sig_shift * (1.0 + shifted * (1.0 - sig_shift)) * scale_ref[...] * mask
    f_val[...] = sig_gate * mask
    f_gate[...] = value * sig_gate * (1.0 - sig_gate) * mask

    def z_part(to, peer, slot):
        return z_copy(1 + to, zsend.at[to, peer], zrecv.at[to], peer, slot)

    def z_stream(peer, slot):
        return z_copy(3, wsend.at[peer], wrecv, peer, slot)

    for to in range(2):
        for half in range(2):

            def s2_wait(o, half=half, to=to):
                slot = lax.rem(lines[half] + o, 4)
                s2_copy(half, to, slot, slot).wait_recv()

            steps(1, 4, s2_wait)
            total = part_in[half, to, 0].astype(F32)
            for q in range(1, 4):
                total += part_in[half, to, q].astype(F32)
            fg[to * 64 + half * 32 : to * 64 + half * 32 + 32, :] = total.astype(BF16)

        def send_pair(n, to=to):
            got = nt(fg[to * 64 : to * 64 + 64, :], fused[rows_of(n * 256, 256), :])
            got = got.astype(BF16)
            for side in range(2):
                peer = 2 * n + side
                zsend[to, peer] = got[:, side * 128 : side * 128 + 128]

                @pl.when(peer != c)
                def _():
                    z_part(to, peer, c).start()

        for o in (2, 1, 3, 0):
            send_pair(lax.rem(lax.div(c, 2) + o, 4))
        zrecv[to, c] = zsend[to, c]

    def z_sum(copy, into):
        def hold(o):
            slot = lax.rem(c + o, NZ)
            copy(slot, slot).wait_recv()

        steps(1, NZ, hold)
        total = into[0].astype(F32)
        for b in range(1, NZ):
            total += into[b].astype(F32)
        return total

    def back_copy(kind, half, to, q, slot):
        if half == 0:
            device = y * RING + q * NCORE + to
        else:
            device = q * RING + x * NCORE + to
        return pltpu.make_async_remote_copy(
            src_ref=owned.at[kind, rows_of(to * 64 + half * 32 + q * 8, 8), :],
            dst_ref=back.at[kind, rows_of(group(half, slot) * 8, 8), :],
            send_sem=b_send.at[kind, half, to * 4 + q],
            recv_sem=b_recv.at[kind, half, slot],
            device_id=(device, c),
            device_id_type=MESH,
        )

    def give_back(kind, to):
        def go(o):
            for half in range(2):
                q = lax.rem(lines[1 - half] + o, 4)
                back_copy(kind, half, to, q, positions[half]).start()

        for o in (2, 1, 3):
            go(o)

        @pl.when(core != to)
        def _():
            for half in range(2):
                back_copy(kind, half, to, lines[1 - half], positions[half]).start()

        @pl.when(core == to)
        def _():
            for half in range(2):
                mine = rows_of(to * 64 + half * 32 + lines[1 - half] * 8, 8)
                home = rows_of(group(half, positions[half]) * 8, 8)
                back[kind, home, :] = owned[kind, mine, :]

    def back_wait(kind, other):
        def hold(o):
            for half in range(2):
                slot = lax.rem(lines[1 - half] + o, 4) * NCORE + other
                back_copy(kind, half, 0, 0, slot).wait_recv()

        steps(1, 4, hold)

        @pl.when(core != other)
        def _():
            for half in range(2):
                back_copy(kind, half, 0, 0, lines[1 - half] * NCORE + other).wait_recv()

    def last_copy(turn, peer, slot):
        rows = slice(0, 48) if turn == 0 else slice(48, 128)
        return pltpu.make_async_remote_copy(
            src_ref=fsend.at[peer, rows, :],
            dst_ref=frecv.at[slot, rows, :],
            send_sem=z_send.at[4 + turn, peer],
            recv_sem=z_recv.at[4 + turn, slot],
            device_id=(me, peer),
            device_id_type=MESH,
        )

    def last_part(turn):
        lo, hi = (0, 48) if turn == 0 else (48, 128)
        new = slice(turn * 64, turn * 64 + 64)
        pad[8 + turn * 64 : 72 + turn * 64, :] = back[0, new, :] * f_gsw[new, :]
        grad_glu = jnp.zeros((hi - lo, 128), F32)
        for k in range(9):
            grad_glu += taps[k : k + 1, :] * pad[12 - k + lo : 12 - k + hi, :]
        grad_expanded = jnp.concatenate(
            [grad_glu * f_val[lo:hi, :], grad_glu * f_gate[lo:hi, :]], axis=1
        ).astype(BF16)
        for o in (2, 1, 3, 0):
            n = lax.rem(lax.div(c, 2) + o, 4)
            got = nt(grad_expanded, expand[rows_of(n * 256, 256), :]).astype(BF16)
            for side in range(2):
                peer = 2 * n + side
                fsend[peer, lo:hi, :] = got[:, side * 128 : side * 128 + 128]

                @pl.when(peer != c)
                def _():
                    last_copy(turn, peer, c).start()

    def early():
        back_wait(0, 0)
        last_part(0)

    pl.when(core == 1)(early)

    for n in range(4):
        got = nt(fg[...], adapter[n * 256 : (n + 1) * 256, :]).astype(BF16)
        wsend[2 * n] = got[:, :128]
        wsend[2 * n + 1] = got[:, 128:]
    for o in FAR_FIRST:
        z_stream(lax.rem(c + o, NZ), c).start()
    wrecv[c] = wsend[c]

    for to in range(2):
        owned[0, to * 64 : to * 64 + 64, :] = z_sum(
            lambda peer, slot, to=to: z_part(to, peer, slot), zrecv.at[to]
        )
        give_back(0, to)
    pl.when(core == 0)(early)
    back_wait(0, 1)
    last_part(1)
    frecv[c] = fsend[c]

    owned[1] = z_sum(z_stream, wrecv)
    for to in range(2):
        give_back(1, to)
    for other in range(2):
        back_wait(1, other)
    stream_out[...] = back[1] * mask

    for turn in range(2):
        lo, hi = (0, 48) if turn == 0 else (48, 128)

        def last_wait(o, turn=turn):
            slot = lax.rem(c + o, NZ)
            last_copy(turn, slot, slot).wait_recv()

        steps(1, NZ, last_wait)
        total = frecv[0, lo:hi, :].astype(F32)
        for b in range(1, NZ):
            total += frecv[b, lo:hi, :].astype(F32)
        normed_out[lo:hi, :] = total

    def sent(o):
        peer = lax.rem(c + o, NZ)
        x_copy(peer, c).wait_send()
        z_stream(peer, c).wait_send()
        for turn in range(2):
            z_part(turn, peer, c).wait_send()
            last_copy(turn, peer, c).wait_send()
        for half in range(2):
            g = lax.rem(positions[half] + o, RING)
            s1_copy(half, g, positions[half]).wait_send()
            id_copy(half, g, positions[half]).wait_send()

    steps(1, NZ, sent)

    def sent_line(o):
        for half in range(2):
            for to in range(2):
                s2_copy(half, to, lax.rem(lines[half] + o, 4), lines[half]).wait_send()
                q = lax.rem(lines[1 - half] + o, 4)
                for kind in range(2):
                    back_copy(kind, half, to, q, positions[half]).wait_send()

    steps(1, 4, sent_line)
    for to in range(2):

        @pl.when(core != to)
        def _():
            for half in range(2):
                for kind in range(2):
                    back_copy(kind, half, to, lines[1 - half], positions[half]).wait_send()


def body(
    frame_cotangent,
    rollout_utterance,
    frame_offset,
    utterance_frames,
    normed_input,
    expand_weight,
    depth_kernel,
    norm_scale,
    norm_shift,
    project_weight,
    adapter_weight,
):
    vmem = pl.BlockSpec(memory_space=pltpu.VMEM)
    hbm = pl.BlockSpec(memory_space=pl.ANY)
    dma = pltpu.SemaphoreType.DMA
    block = jax.ShapeDtypeStruct((128, 128), F32)
    stream, normed = pl.pallas_call(
        kernel,
        out_shape=(block, block),
        in_specs=[hbm] * 11,
        out_specs=(vmem, vmem),
        scratch_shapes=[
            pltpu.SMEM((8,), jnp.int32),
            pltpu.SMEM((8,), jnp.int32),
            pltpu.SMEM((1,), jnp.int32),
            pltpu.VMEM((128, 128), BF16),
            pltpu.VMEM((9, 128), BF16),
            pltpu.VMEM((1, 128), F32),
            pltpu.VMEM((1, 128), F32),
            pltpu.VMEM((8, 160, 1024), BF16),
            pltpu.VMEM((2048, 128), BF16),
            pltpu.VMEM((1024, 1024), BF16),
            pltpu.VMEM((1024, 1024), BF16),
            pltpu.VMEM((1024, 1024), BF16),
            pltpu.VMEM((1024, 256), BF16),
            pltpu.VMEM((16, 64, 1024), BF16),
            pltpu.VMEM((2, 8, 64, 1024), BF16),
            pltpu.VMEM((2, 8, 8, 128), jnp.int32),
            pltpu.VMEM((512, 256), F32),
            pltpu.VMEM((2, 256, 512), BF16),
            pltpu.VMEM((2, 4, 2, 32, 1024), BF16),
            pltpu.VMEM((2, 2, 4, 32, 1024), BF16),
            pltpu.VMEM((128, 1024), BF16),
            pltpu.VMEM((8, 128, 128), BF16),
            pltpu.VMEM((2, 8, 64, 128), BF16),
            pltpu.VMEM((2, 8, 64, 128), BF16),
            pltpu.VMEM((8, 128, 128), BF16),
            pltpu.VMEM((8, 128, 128), BF16),
            pltpu.VMEM((8, 128, 128), BF16),
            pltpu.VMEM((8, 128, 128), BF16),
            pltpu.VMEM((2, 128, 128), F32),
            pltpu.VMEM((2, 128, 128), F32),
            pltpu.VMEM((144, 128), F32),
            pltpu.VMEM((128, 128), F32),
            pltpu.VMEM((128, 128), F32),
            pltpu.VMEM((128, 128), F32),
            dma((14,)),
            dma((2, 8)),
            dma((2, 8)),
            dma((2, 8)),
            dma((2, 8)),
            dma((2, 2, 4)),
            dma((2, 2, 4)),
            dma((6, 8)),
            dma((6, 8)),
            dma((2, 2, 8)),
            dma((2, 2, 8)),
        ],
        compiler_params=pltpu.CompilerParams(
            collective_id=0, has_side_effects=True, vmem_limit_bytes=63 * 1024 * 1024
        ),
        cost_estimate=pl.CostEstimate(
            flops=5_000_000_000, bytes_accessed=8_000_000, transcendentals=40_000
        ),
    )(
        rollout_utterance,
        frame_offset,
        utterance_frames,
        normed_input.reshape(128, 128),
        depth_kernel,
        norm_scale.reshape(1, 128),
        norm_shift.reshape(1, 128),
        frame_cotangent,
        expand_weight.reshape(2048, 128),
        project_weight,
        adapter_weight,
    )
    stream, normed = lax.optimization_barrier((stream, normed))
    return stream.reshape(1, 128, 128).astype(BF16), normed.reshape(1, 128, 128).astype(BF16)


def solution(mesh):
    return jax.shard_map(
        body,
        mesh=mesh,
        in_specs=(
            P("dec", None, "ch"),
            P("dec"),
            P("dec"),
            P("dec"),
            P("dec", None, "ch"),
            P(None, None, "ch"),
            P(None, "ch"),
            P("ch"),
            P("ch"),
            P(),
            P(None, "ch"),
        ),
        out_specs=(P("dec", None, "ch"), P("dec", None, "ch")),
        check_vma=False,
    )
```

```python
import jax
import jax.numpy as jnp
from jax import lax
from jax.experimental import pallas as pl
from jax.experimental.pallas import tpu as pltpu
from jax.sharding import PartitionSpec as P

MESH = pl.DeviceIdType.MESH
F32 = jnp.float32
BF16 = jnp.bfloat16
NY, NX, NCORE, NZ = 4, 4, 2, 8
FAR_FIRST = (4, 3, 5, 2, 6, 1, 7)
RING = NX * NCORE


def steps(first, last, work):
    def one(step, carry):
        work(step)
        return carry

    lax.fori_loop(first, last, one, 0)


def rows_of(start, size):
    return pl.ds(pl.multiple_of(start, size), size)


def nt(a, b):
    return lax.dot_general(a, b, (((1,), (1,)), ((), ())), preferred_element_type=F32)


def kernel(
    ids_hbm,
    offs_hbm,
    frames_hbm,
    normed_hbm,
    taps_hbm,
    scale_hbm,
    shift_hbm,
    cot_hbm,
    expand_hbm,
    project_hbm,
    adapter_hbm,
    stream_out,
    normed_out,
    ids_sm,
    offs_sm,
    frames_sm,
    normed_ref,
    taps_ref,
    scale_ref,
    shift_ref,
    cot,
    expand2,
    project,
    adapter,
    fused,
    expand,
    slabs,
    landed,
    ids,
    sel_t,
    sel,
    part,
    part_in,
    fg,
    x_all,
    zsend,
    zrecv,
    wsend,
    wrecv,
    fsend,
    frecv,
    owned,
    back,
    pad,
    f_gsw,
    f_val,
    f_gate,
    load_sem,
    s1_send,
    s1_recv,
    id_send,
    id_recv,
    s2_send,
    s2_recv,
    z_send,
    z_recv,
    b_send,
    b_recv,
):
    me = lax.axis_index("dec")
    c = lax.axis_index("ch")
    y = lax.div(me, RING)
    pos_a = lax.rem(me, RING)
    x = lax.div(pos_a, NCORE)
    core = lax.rem(pos_a, NCORE)
    pos_b = y * NCORE + core
    positions = (pos_a, pos_b)

    def group(half, g):
        return lax.rem(g, NCORE) * 8 + half * 4 + lax.div(g, NCORE)

    def ring_dev(half, g):
        if half == 0:
            return y * RING + g
        return lax.div(g, NCORE) * RING + x * NCORE + lax.rem(g, NCORE)

    def line_dev(half, q):
        if half == 0:
            return q * RING + pos_a
        return y * RING + q * NCORE + core

    lines = (y, x)

    small = (
        (offs_hbm, offs_sm),
        (ids_hbm, ids_sm),
        (normed_hbm, normed_ref),
        (frames_hbm, frames_sm),
        (taps_hbm, taps_ref),
        (scale_hbm, scale_ref),
        (shift_hbm, shift_ref),
    )
    pairs = [(cot_hbm.at[2 * p : 2 * p + 2], cot.at[2 * p : 2 * p + 2]) for p in range(4)]
    pairs += [(project_hbm, project), (adapter_hbm, adapter), (expand_hbm, expand2)]
    pairs += small
    loads = [pltpu.make_async_copy(a, b, load_sem.at[n]) for n, (a, b) in enumerate(pairs)]
    for n in (7, 8, 0, 1, 2, 3):
        loads[n].start()

    barrier = pltpu.get_barrier_semaphore()

    def greet(device):
        pl.semaphore_signal(barrier, inc=1, device_id=device, device_id_type=MESH)

    steps(1, RING, lambda o: greet((ring_dev(0, lax.rem(pos_a + o, RING)), c)))
    for other in range(NCORE):
        steps(1, NY, lambda o: greet((ring_dev(1, lax.rem(y + o, NY) * NCORE + other), c)))
    steps(1, NZ, lambda o: greet((me, lax.rem(c + o, NZ))))

    for n in (9, 4, 5, 6, 10, 11, 12, 13):
        loads[n].start()
    loads[7].wait()
    loads[8].wait()
    row8 = lax.broadcasted_iota(jnp.int32, (8, 128), 0)
    tile = jnp.zeros((8, 128), jnp.int32)
    for r in range(8):
        tile = jnp.where(row8 == r, ids_sm[r], tile)
    ids[0, pos_a] = tile
    ids[1, pos_b] = tile

    srow = lax.broadcasted_iota(jnp.int32, (128, 160), 0)
    scol = lax.broadcasted_iota(jnp.int32, (128, 160), 1)
    diff = scol - srow
    for p in range(4):
        loads[p].wait()
        sh0 = (diff == offs_sm[2 * p]).astype(F32).astype(BF16)
        sh1 = (diff == offs_sm[2 * p + 1]).astype(F32).astype(BF16)
        for n in range(4):
            cols = slice(n * 256, (n + 1) * 256)
            a = jnp.dot(sh0, cot[2 * p, :, cols], preferred_element_type=F32)
            b = jnp.dot(sh1, cot[2 * p + 1, :, cols], preferred_element_type=F32)
            both = jnp.concatenate([a.reshape(16, 8, 256), b.reshape(16, 8, 256)], axis=1)
            slabs[:, p * 16 : (p + 1) * 16, cols] = both.astype(BF16)

    pl.semaphore_wait(barrier, 20)

    def s1_copy(half, g, slot):
        return pltpu.make_async_remote_copy(
            src_ref=slabs.at[group(half, g)],
            dst_ref=landed.at[half, slot],
            send_sem=s1_send.at[half, g],
            recv_sem=s1_recv.at[half, slot],
            device_id=(ring_dev(half, g), c),
            device_id_type=MESH,
        )

    def id_copy(half, g, slot):
        return pltpu.make_async_remote_copy(
            src_ref=ids.at[half, positions[half]],
            dst_ref=ids.at[half, slot],
            send_sem=id_send.at[half, g],
            recv_sem=id_recv.at[half, slot],
            device_id=(ring_dev(half, g), c),
            device_id_type=MESH,
        )

    def id_start(o):
        for half in range(2):
            g = lax.rem(positions[half] + o, RING)
            id_copy(half, g, positions[half]).start()

    def s1_out(other, offsets):
        for o in offsets:
            for half in range(2):
                g = lax.rem(lines[1 - half] + o, 4) * NCORE + other
                s1_copy(half, g, positions[half]).start()

    def s1_beside(other):
        for half in range(2):
            s1_copy(half, lines[1 - half] * NCORE + other, positions[half]).start()

    s1_out(0, (2,))
    steps(1, RING, id_start)
    s1_out(0, (1, 3))
    pl.when(core == 1)(lambda: s1_beside(0))
    s1_out(1, (1, 3))

    @pl.when(core == 1)
    def _():
        s1_out(1, (2,))

    @pl.when(core == 0)
    def _():
        s1_beside(1)

    def z_copy(turn, src, dst, peer, slot):
        return pltpu.make_async_remote_copy(
            src_ref=src,
            dst_ref=dst.at[slot],
            send_sem=z_send.at[turn, peer],
            recv_sem=z_recv.at[turn, slot],
            device_id=(me, peer),
            device_id_type=MESH,
        )

    def x_copy(peer, slot):
        return z_copy(0, normed_ref, x_all, peer, slot)

    loads[9].wait()
    for o in FAR_FIRST:
        x_copy(lax.rem(c + o, NZ), c).start()
    x_all[c] = normed_ref[...]
    for half in range(2):
        landed[half, positions[half]] = slabs[group(half, positions[half])]

    loads[4].wait()
    loads[5].wait()

    def fuse(i):
        mine = rows_of(i * 128, 128)
        for n in range(4):
            cols = slice(n * 256, (n + 1) * 256)
            fused[mine, cols] = jnp.dot(
                project[mine, :], adapter[:, cols], preferred_element_type=F32
            ).astype(BF16)

    steps(0, 8, fuse)

    loads[6].wait()
    for n in range(10, 14):
        loads[n].wait()
    prow = lax.broadcasted_iota(jnp.int32, (256, 256), 0)
    pcol = lax.broadcasted_iota(jnp.int32, (256, 256), 1)
    want = jnp.where(prow < 128, 2 * prow, 2 * prow - 255)
    apart = (pcol == want).astype(F32).astype(BF16)
    for b in range(8):
        both = jnp.dot(apart, expand2[b * 256 : (b + 1) * 256, :], preferred_element_type=F32)
        both = both.astype(BF16)
        expand[b * 128 : (b + 1) * 128, 0:128] = both[:128]
        expand[b * 128 : (b + 1) * 128, 128:256] = both[128:]

    lane = lax.broadcasted_iota(jnp.int32, (8, 256), 1)
    same = lax.broadcasted_iota(jnp.int32, (8, 256), 0) == lax.rem(lane, 8)
    unit = lax.div(lane, 8)
    outer = lax.rem(lax.div(unit, 4), 4)
    inner = lax.rem(unit, 4)
    odd = lax.div(unit, 16)
    utts = ((outer * NX + inner) * NCORE + odd, (inner * NX + outer) * NCORE + odd)
    for half in range(2):

        def id_wait(o, half=half):
            slot = lax.rem(positions[half] + o, RING)
            id_copy(half, slot, slot).wait_recv()

        steps(1, RING, id_wait)

        def choose(s, half=half):
            for r in range(8):
                row = ids[half, s, r : r + 1, :]
                wide = jnp.concatenate([row, row], axis=1)
                hit = jnp.logical_and(same, wide == utts[half])
                sel_t[rows_of(s * 64 + r * 8, 8), :] = hit.astype(F32)

        steps(0, 8, choose)
        sel[half] = sel_t[...].T.astype(BF16)

    def s2_copy(half, to, q, slot):
        return pltpu.make_async_remote_copy(
            src_ref=part.at[half, q, to],
            dst_ref=part_in.at[half, to, slot],
            send_sem=s2_send.at[half, to, q],
            recv_sem=s2_recv.at[half, to, slot],
            device_id=(line_dev(half, q), c),
            device_id_type=MESH,
        )

    for to in range(2):
        for half in range(2):
            if to == 0:

                def s1_wait(o, half=half):
                    slot = lax.rem(positions[half] + o, RING)
                    s1_copy(half, slot, slot).wait_recv()

                steps(1, RING, s1_wait)
            for n in range(4):
                cols = slice(n * 256, (n + 1) * 256)
                got = jnp.dot(
                    sel[half, to * 128 : to * 128 + 128, :],
                    landed[half, :, :, cols].reshape(512, 256),
                    preferred_element_type=F32,
                )
                part[half, :, to, :, cols] = got.astype(BF16).reshape(4, 32, 256)
            for o in (2, 1, 3):
                s2_copy(half, to, lax.rem(lines[half] + o, 4), lines[half]).start()
            part_in[half, to, lines[half]] = part[half, lines[half], to]

    @pl.when(core == 0)
    def _():
        s1_out(1, (2,))


    steps(1, NZ, lambda o: x_copy(lax.rem(c + o, NZ), lax.rem(c + o, NZ)).wait_recv())
    both = jnp.zeros((128, 256), F32)
    for b in range(8):
        both += jnp.dot(
            x_all[b], expand[b * 128 : (b + 1) * 128, :], preferred_element_type=F32
        )
    value = both[:, :128]
    sig_gate = jax.nn.sigmoid(both[:, 128:])
    frame = lax.broadcasted_iota(jnp.int32, (128, 128), 0)
    mask = (frame < frames_sm[0]).astype(F32)
    pad[...] = jnp.zeros_like(pad)
    pad[8:136, :] = mask * value * sig_gate
    taps = taps_ref[...].astype(F32)
    depth = jnp.zeros((128, 128), F32)
    for k in range(9):
        depth += taps[k : k + 1, :] * pad[4 + k : 132 + k, :]
    shifted = depth * scale_ref[...] + shift_ref[...]
    sig_shift = jax.nn.sigmoid(shifted)
    f_gsw[...] = sig_shift * (1.0 + shifted * (1.0 - sig_shift)) * scale_ref[...] * mask
    f_val[...] = sig_gate * mask
    f_gate[...] = value * sig_gate * (1.0 - sig_gate) * mask

    def z_part(to, peer, slot):
        return z_copy(1 + to, zsend.at[to, peer], zrecv.at[to], peer, slot)

    def z_stream(peer, slot):
        return z_copy(3, wsend.at[peer], wrecv, peer, slot)

    for to in range(2):
        for half in range(2):

            def s2_wait(o, half=half, to=to):
                slot = lax.rem(lines[half] + o, 4)
                s2_copy(half, to, slot, slot).wait_recv()

            steps(1, 4, s2_wait)
            total = part_in[half, to, 0].astype(F32)
            for q in range(1, 4):
                total += part_in[half, to, q].astype(F32)
            fg[to * 64 + half * 32 : to * 64 + half * 32 + 32, :] = total.astype(BF16)

        def send_pair(n, to=to):
            got = nt(fg[to * 64 : to * 64 + 64, :], fused[rows_of(n * 256, 256), :])
            got = got.astype(BF16)
            for side in range(2):
                peer = 2 * n + side
                zsend[to, peer] = got[:, side * 128 : side * 128 + 128]

                @pl.when(peer != c)
                def _():
                    z_part(to, peer, c).start()

        for o in (2, 1, 3, 0):
            send_pair(lax.rem(lax.div(c, 2) + o, 4))
        zrecv[to, c] = zsend[to, c]

    def z_sum(copy, into):
        def hold(o):
            slot = lax.rem(c + o, NZ)
            copy(slot, slot).wait_recv()

        steps(1, NZ, hold)
        total = into[0].astype(F32)
        for b in range(1, NZ):
            total += into[b].astype(F32)
        return total

    def back_copy(kind, half, to, q, slot):
        if half == 0:
            device = y * RING + q * NCORE + to
        else:
            device = q * RING + x * NCORE + to
        return pltpu.make_async_remote_copy(
            src_ref=owned.at[kind, rows_of(to * 64 + half * 32 + q * 8, 8), :],
            dst_ref=back.at[kind, rows_of(group(half, slot) * 8, 8), :],
            send_sem=b_send.at[kind, half, to * 4 + q],
            recv_sem=b_recv.at[kind, half, slot],
            device_id=(device, c),
            device_id_type=MESH,
        )

    def give_back(kind, to):
        def go(o):
            for half in range(2):
                q = lax.rem(lines[1 - half] + o, 4)
                back_copy(kind, half, to, q, positions[half]).start()

        for o in (2, 1, 3):
            go(o)

        @pl.when(core != to)
        def _():
            for half in range(2):
                back_copy(kind, half, to, lines[1 - half], positions[half]).start()

        @pl.when(core == to)
        def _():
            for half in range(2):
                mine = rows_of(to * 64 + half * 32 + lines[1 - half] * 8, 8)
                home = rows_of(group(half, positions[half]) * 8, 8)
                back[kind, home, :] = owned[kind, mine, :]

    def back_wait(kind, other):
        def hold(o):
            for half in range(2):
                slot = lax.rem(lines[1 - half] + o, 4) * NCORE + other
                back_copy(kind, half, 0, 0, slot).wait_recv()

        steps(1, 4, hold)

        @pl.when(core != other)
        def _():
            for half in range(2):
                back_copy(kind, half, 0, 0, lines[1 - half] * NCORE + other).wait_recv()

    def last_copy(turn, peer, slot):
        rows = slice(0, 48) if turn == 0 else slice(48, 128)
        return pltpu.make_async_remote_copy(
            src_ref=fsend.at[peer, rows, :],
            dst_ref=frecv.at[slot, rows, :],
            send_sem=z_send.at[4 + turn, peer],
            recv_sem=z_recv.at[4 + turn, slot],
            device_id=(me, peer),
            device_id_type=MESH,
        )

    def last_part(turn):
        lo, hi = (0, 48) if turn == 0 else (48, 128)
        new = slice(turn * 64, turn * 64 + 64)
        pad[8 + turn * 64 : 72 + turn * 64, :] = back[0, new, :] * f_gsw[new, :]
        grad_glu = jnp.zeros((hi - lo, 128), F32)
        for k in range(9):
            grad_glu += taps[k : k + 1, :] * pad[12 - k + lo : 12 - k + hi, :]
        grad_expanded = jnp.concatenate(
            [grad_glu * f_val[lo:hi, :], grad_glu * f_gate[lo:hi, :]], axis=1
        ).astype(BF16)
        for o in (2, 1, 3, 0):
            n = lax.rem(lax.div(c, 2) + o, 4)
            got = nt(grad_expanded, expand[rows_of(n * 256, 256), :]).astype(BF16)
            for side in range(2):
                peer = 2 * n + side
                fsend[peer, lo:hi, :] = got[:, side * 128 : side * 128 + 128]

                @pl.when(peer != c)
                def _():
                    last_copy(turn, peer, c).start()

    def early():
        back_wait(0, 0)
        last_part(0)


    for n in range(4):
        got = nt(fg[...], adapter[n * 256 : (n + 1) * 256, :]).astype(BF16)
        wsend[2 * n] = got[:, :128]
        wsend[2 * n + 1] = got[:, 128:]
    for o in FAR_FIRST:
        z_stream(lax.rem(c + o, NZ), c).start()
    wrecv[c] = wsend[c]

    for to in range(2):
        owned[0, to * 64 : to * 64 + 64, :] = z_sum(
            lambda peer, slot, to=to: z_part(to, peer, slot), zrecv.at[to]
        )
        give_back(0, to)
    early()
    back_wait(0, 1)
    last_part(1)
    frecv[c] = fsend[c]

    owned[1] = z_sum(z_stream, wrecv)
    for to in range(2):
        give_back(1, to)
    for other in range(2):
        back_wait(1, other)
    stream_out[...] = back[1] * mask

    for turn in range(2):
        lo, hi = (0, 48) if turn == 0 else (48, 128)

        def last_wait(o, turn=turn):
            slot = lax.rem(c + o, NZ)
            last_copy(turn, slot, slot).wait_recv()

        steps(1, NZ, last_wait)
        total = frecv[0, lo:hi, :].astype(F32)
        for b in range(1, NZ):
            total += frecv[b, lo:hi, :].astype(F32)
        normed_out[lo:hi, :] = total

    def sent(o):
        peer = lax.rem(c + o, NZ)
        x_copy(peer, c).wait_send()
        z_stream(peer, c).wait_send()
        for turn in range(2):
            z_part(turn, peer, c).wait_send()
            last_copy(turn, peer, c).wait_send()
        for half in range(2):
            g = lax.rem(positions[half] + o, RING)
            s1_copy(half, g, positions[half]).wait_send()
            id_copy(half, g, positions[half]).wait_send()

    steps(1, NZ, sent)

    def sent_line(o):
        for half in range(2):
            for to in range(2):
                s2_copy(half, to, lax.rem(lines[half] + o, 4), lines[half]).wait_send()
                q = lax.rem(lines[1 - half] + o, 4)
                for kind in range(2):
                    back_copy(kind, half, to, q, positions[half]).wait_send()

    steps(1, 4, sent_line)
    for to in range(2):

        @pl.when(core != to)
        def _():
            for half in range(2):
                for kind in range(2):
                    back_copy(kind, half, to, lines[1 - half], positions[half]).wait_send()


def body(
    frame_cotangent,
    rollout_utterance,
    frame_offset,
    utterance_frames,
    normed_input,
    expand_weight,
    depth_kernel,
    norm_scale,
    norm_shift,
    project_weight,
    adapter_weight,
):
    vmem = pl.BlockSpec(memory_space=pltpu.VMEM)
    hbm = pl.BlockSpec(memory_space=pl.ANY)
    dma = pltpu.SemaphoreType.DMA
    block = jax.ShapeDtypeStruct((128, 128), F32)
    stream, normed = pl.pallas_call(
        kernel,
        out_shape=(block, block),
        in_specs=[hbm] * 11,
        out_specs=(vmem, vmem),
        scratch_shapes=[
            pltpu.SMEM((8,), jnp.int32),
            pltpu.SMEM((8,), jnp.int32),
            pltpu.SMEM((1,), jnp.int32),
            pltpu.VMEM((128, 128), BF16),
            pltpu.VMEM((9, 128), BF16),
            pltpu.VMEM((1, 128), F32),
            pltpu.VMEM((1, 128), F32),
            pltpu.VMEM((8, 160, 1024), BF16),
            pltpu.VMEM((2048, 128), BF16),
            pltpu.VMEM((1024, 1024), BF16),
            pltpu.VMEM((1024, 1024), BF16),
            pltpu.VMEM((1024, 1024), BF16),
            pltpu.VMEM((1024, 256), BF16),
            pltpu.VMEM((16, 64, 1024), BF16),
            pltpu.VMEM((2, 8, 64, 1024), BF16),
            pltpu.VMEM((2, 8, 8, 128), jnp.int32),
            pltpu.VMEM((512, 256), F32),
            pltpu.VMEM((2, 256, 512), BF16),
            pltpu.VMEM((2, 4, 2, 32, 1024), BF16),
            pltpu.VMEM((2, 2, 4, 32, 1024), BF16),
            pltpu.VMEM((128, 1024), BF16),
            pltpu.VMEM((8, 128, 128), BF16),
            pltpu.VMEM((2, 8, 64, 128), BF16),
            pltpu.VMEM((2, 8, 64, 128), BF16),
            pltpu.VMEM((8, 128, 128), BF16),
            pltpu.VMEM((8, 128, 128), BF16),
            pltpu.VMEM((8, 128, 128), BF16),
            pltpu.VMEM((8, 128, 128), BF16),
            pltpu.VMEM((2, 128, 128), F32),
            pltpu.VMEM((2, 128, 128), F32),
            pltpu.VMEM((144, 128), F32),
            pltpu.VMEM((128, 128), F32),
            pltpu.VMEM((128, 128), F32),
            pltpu.VMEM((128, 128), F32),
            dma((14,)),
            dma((2, 8)),
            dma((2, 8)),
            dma((2, 8)),
            dma((2, 8)),
            dma((2, 2, 4)),
            dma((2, 2, 4)),
            dma((6, 8)),
            dma((6, 8)),
            dma((2, 2, 8)),
            dma((2, 2, 8)),
        ],
        compiler_params=pltpu.CompilerParams(
            collective_id=0, has_side_effects=True, vmem_limit_bytes=63 * 1024 * 1024
        ),
        cost_estimate=pl.CostEstimate(
            flops=5_000_000_000, bytes_accessed=8_000_000, transcendentals=40_000
        ),
    )(
        rollout_utterance,
        frame_offset,
        utterance_frames,
        normed_input.reshape(128, 128),
        depth_kernel,
        norm_scale.reshape(1, 128),
        norm_shift.reshape(1, 128),
        frame_cotangent,
        expand_weight.reshape(2048, 128),
        project_weight,
        adapter_weight,
    )
    stream, normed = lax.optimization_barrier((stream, normed))
    return stream.reshape(1, 128, 128).astype(BF16), normed.reshape(1, 128, 128).astype(BF16)


def solution(mesh):
    return jax.shard_map(
        body,
        mesh=mesh,
        in_specs=(
            P("dec", None, "ch"),
            P("dec"),
            P("dec"),
            P("dec"),
            P("dec", None, "ch"),
            P(None, None, "ch"),
            P(None, "ch"),
            P("ch"),
            P("ch"),
            P(),
            P(None, "ch"),
        ),
        out_specs=(P("dec", None, "ch"), P("dec", None, "ch")),
        check_vma=False,
    )
```
